512 devices in a mesh: row: 64 (over z, x, y_hi), col: 8 (over y_lo, core).
Axes of the slice: x: 4, y: 8 (y_hi: 2, y_lo: 4; y = y_hi * 4 + y_lo), z: 8, core: 2. Of those that a mesh axis runs over, the one named last changes fastest.
Arguments:
- row_embed: bfloat16 [256, 256, 256], P('row', 'col')
- col_embed: bfloat16 [32, 256, 256], P('col', 'row')
- row_length: int32 [256], P('row'), may hold values from 32 to 256, as said below
- col_length: int32 [32], P('col'), may hold values from 32 to 256, as said below
- pair_valid: int32 [256, 32], P('row', 'col'), may hold values 0 or 1
- temper: float32 [8], replicated, may hold values from 0.05 to 0.25
- row_vector: float32 [256], replicated, may hold values from -0.375 to 0.375
- col_vector: float32 [256], replicated, may hold values from -0.375 to 0.375
Outputs:
- row_score: float32 [256, 256], P('row', 'col')
- col_score: float32 [32, 256], P('col', 'row')
The draws below stay inside these ranges and needn't reach their ends.
Inputs may be any that keep to these rules, and one draw needn't show every extreme that they name: `row_length`: every length is at least 32; in every draw some row protein and some column protein have exactly 256 residues. `col_length`: every length is at least 32; some column protein has exactly 256 residues.
All inputs are finite; a program needn't handle non-finite values. No bound on the sum of `pair_valid` on one device may be relied on, other than what follows from the above.
Results may differ from the reference program's by a relative error of at most 0.0004.
Values may be sent and summed in bfloat16 or wider, within the bound.
A program may use at most 64 MiB of HBM per device.

```python
import math
import jax
import jax.numpy as jnp
from jax import lax

H = 256
NH = 8
L = 256
ROWS = 256
COLS = 32


def draw_row_embed(key, part):
    key = jax.random.fold_in(key, 1)
    drawn = jnp.clip(jax.random.normal(key, (ROWS, L, H), jnp.float32), -6.0, 6.0)
    return drawn.astype(jnp.bfloat16)


def draw_col_embed(key, part):
    key = jax.random.fold_in(key, 2)
    drawn = jnp.clip(jax.random.normal(key, (COLS, L, H), jnp.float32), -6.0, 6.0)
    return drawn.astype(jnp.bfloat16)


def draw_lengths(key, count):
    drawn = jax.random.randint(key, (count,), L // 8, L + 1)
    longest = jax.random.randint(jax.random.fold_in(key, 9), (), 0, count)
    return drawn.at[longest].set(L).astype(jnp.int32)


def draw_row_length(key, part):
    key = jax.random.fold_in(key, 3)
    return draw_lengths(key, ROWS)


def draw_col_length(key, part):
    key = jax.random.fold_in(key, 4)
    return draw_lengths(key, COLS)


def place_ends(values, rng, least, top_value):
    spot = [jax.random.randint(jax.random.fold_in(rng, axis), (), 0, length) for axis, length in enumerate(values.shape)]
    widest = values.shape.index(max(values.shape))
    next_to = spot[:widest] + [(spot[widest] + 1) % values.shape[widest]] + spot[widest + 1:]
    return values.at[tuple(spot)].set(least).at[tuple(next_to)].set(top_value)


def bell_draw(own_key, dims, width, bound, held_as=jnp.bfloat16):
    values = jax.random.normal(own_key, dims, jnp.float32) * width
    return jnp.minimum(jnp.maximum(values, -bound), bound).astype(held_as)


def setup_inputs(seed: int = 0) -> dict:
    seeds = jax.random.split(jax.random.key(seed), 9)
    return {
        "row_embed": draw_row_embed(jax.random.fold_in(seeds[8], 71), 0),
        "col_embed": draw_col_embed(jax.random.fold_in(seeds[8], 71), 0),
        "row_length": draw_row_length(jax.random.fold_in(seeds[8], 71), 0),
        "col_length": draw_col_length(jax.random.fold_in(seeds[8], 71), 0),
        "pair_valid": place_ends((jax.random.randint(seeds[4], (ROWS, COLS), 0, 4) < 3).astype(jnp.int32), jax.random.fold_in(seeds[4], 1), 0, 1),
        "temper": jnp.clip(jnp.exp(jax.random.uniform(seeds[5], (NH,), jnp.float32, math.log(0.05), math.log(0.25))), 0.05, 0.25),
        "row_vector": bell_draw(seeds[6], (H,), H ** -0.5, 0.375, jnp.float32),
        "col_vector": bell_draw(seeds[7], (H,), H ** -0.5, 0.375, jnp.float32),
    }


far_below = -1e+30

def split_heads(block_rows, head_count):
    return block_rows.reshape(block_rows.shape[0], head_count, block_rows.shape[1] // head_count)

def pair_scores(query_rows, key_rows, temper):
    head_count = temper.shape[0]
    raw_scores = jnp.einsum('ahd,bhd->hab', split_heads(query_rows, head_count).astype(jnp.float32), split_heads(key_rows, head_count).astype(jnp.float32))
    return raw_scores * temper[:, None, None]

def weights_along(scores, valid_mask, along_axis):
    masked = jnp.where(valid_mask, scores, far_below)
    peak_value = lax.optimization_barrier(jnp.max(masked, axis=along_axis, keepdims=True))
    raised = jnp.where(valid_mask, jnp.exp(masked - peak_value), 0.0)
    return (raised / lax.optimization_barrier(jnp.sum(raised, axis=along_axis, keepdims=True))).astype(jnp.bfloat16)

def readout(attended, own_rows, vector):
    return lax.optimization_barrier(jnp.sum(jnp.tanh(attended + own_rows.astype(jnp.float32)) * vector, axis=-1))

def pair_terms(query_rows, key_rows, row_len, col_len, temper, row_vector, col_vector):
    head_count = temper.shape[0]
    scores = pair_scores(query_rows, key_rows, temper)
    row_pos = jnp.arange(query_rows.shape[0])
    col_pos = jnp.arange(key_rows.shape[0])
    toward_cols = weights_along(scores, (col_pos < col_len)[None, None, :], 2)
    toward_rows = weights_along(scores, (row_pos < row_len)[None, :, None], 1)
    row_out = jnp.einsum('hab,bhd->ahd', toward_cols.astype(jnp.float32), split_heads(key_rows, head_count).astype(jnp.float32)).reshape(query_rows.shape)
    col_out = jnp.einsum('hab,ahd->bhd', toward_rows.astype(jnp.float32), split_heads(query_rows, head_count).astype(jnp.float32)).reshape(key_rows.shape)
    row_term = jnp.where(row_pos < row_len, readout(row_out, query_rows, row_vector), 0.0)
    col_term = jnp.where(col_pos < col_len, readout(col_out, key_rows, col_vector), 0.0)
    return (row_term, col_term)

def reference(row_embed, col_embed, row_length, col_length, pair_valid, temper, row_vector, col_vector):

    def one_row(col_total, inputs):
        row_one, row_len, valid_row = inputs
        row_terms, col_terms = jax.vmap(lambda col_one, col_len: pair_terms(row_one, col_one, row_len, col_len, temper, row_vector, col_vector))(col_embed, col_length)
        weight = valid_row.astype(jnp.float32)
        row_total = lax.optimization_barrier(jnp.sum(row_terms * weight[:, None], axis=0))
        return (col_total + col_terms * weight[:, None], row_total)
    start_total = jnp.zeros((COLS, L), jnp.float32)
    col_total, row_total = lax.scan(one_row, start_total, (row_embed, row_length, pair_valid))
    return (row_total * (1.0 / math.sqrt(COLS)), col_total * (1.0 / math.sqrt(ROWS)))
```

```python
import functools
import math

import jax
import jax.numpy as jnp
from jax import lax
from jax.experimental import pallas as pl
from jax.experimental.pallas import tpu as pltpu
from jax.sharding import PartitionSpec as P

MESH = pl.DeviceIdType.MESH
f32 = jnp.float32
bf16 = jnp.bfloat16
LOG2E = math.log2(math.e)

N_ROW = 64
N_COL = 8
R = 4
C = 4
L = 256
H = 256
NH = 8
D = H // NH
HT = 128 // D
STEPS = 2 * (C // 2) * R


def dot(a, b):
    return jnp.dot(a, b, preferred_element_type=f32)


def dot_t(a, b):
    return lax.dot_general(a, b, (((1,), (1,)), ((), ())), preferred_element_type=f32)


def kernel(
    row_hbm, col_in, row_len, col_len, valid, temper, row_vec, col_vec,
    row_out, col_out,
    col_own, row_buf, col_buf, col_nat,
    ql, kt, qt, vt, qf, kf, rv, cv,
    scores, e_row, e_col, row_acc, col_acc,
    row_res, row_got, col_msg, col_got,
    row_send, row_recv, col_send, col_recv, rres_send, rres_recv, cres_send, cres_recv,
):
    r = lax.axis_index("row")
    c = lax.axis_index("col")

    def row_peer(k):
        return (lax.rem(r + k, N_ROW), c)

    def col_peer(k):
        return (r, lax.rem(c + k, N_COL))

    barrier = pltpu.get_barrier_semaphore()

    def greet_row(k, _):
        pl.semaphore_signal(barrier, inc=1, device_id=row_peer(k), device_id_type=MESH)
        return 0

    def greet_col(k, _):
        pl.semaphore_signal(barrier, inc=1, device_id=col_peer(k), device_id_type=MESH)
        return 0

    lax.fori_loop(1, N_ROW, greet_row, 0)
    lax.fori_loop(1, N_COL, greet_col, 0)

    for j in range(C):
        kf[0, j, 0:4, 0:H] = col_in[j].astype(f32)
    for t in range(2):
        own = jnp.concatenate([kf[0, j, 0:4, t * 128:(t + 1) * 128] for j in range(C)], axis=0)
        col_own[t] = own.astype(bf16)

    rv[...] = jnp.broadcast_to(row_vec[...], (L, H)).T.reshape(NH, D, L)
    cv[...] = jnp.broadcast_to(col_vec[...], (L, H)).T.reshape(NH, D, L)
    row_acc[...] = jnp.zeros_like(row_acc)
    col_acc[...] = jnp.zeros_like(col_acc)

    pl.semaphore_wait(barrier, N_ROW - 1 + N_COL - 1)

    own_rows = pl.ds(pl.multiple_of(c * 32, 32), 32)
    for t in range(2):
        half = pl.ds(t * 128, 128)

        def send_col(k, _):
            pltpu.make_async_remote_copy(
                src_ref=col_own.at[t], dst_ref=col_buf.at[t, r],
                send_sem=col_send, recv_sem=col_recv.at[t],
                device_id=row_peer(k), device_id_type=MESH).start()
            return 0

        def send_row(k, _):
            pltpu.make_async_remote_copy(
                src_ref=row_hbm.at[:, :, half], dst_ref=row_buf.at[t, :, own_rows, :],
                send_sem=row_send, recv_sem=row_recv.at[t],
                device_id=col_peer(k), device_id_type=MESH).start()
            return 0

        lax.fori_loop(1, N_COL, send_row, 0)
        lax.fori_loop(1, N_ROW, send_col, 0)
        pltpu.make_async_copy(row_hbm.at[:, :, half], row_buf.at[t, :, own_rows, :], row_recv.at[t]).start()
        pltpu.make_async_copy(col_own.at[t], col_buf.at[t, r], col_recv.at[t]).start()

    lane = lax.broadcasted_iota(jnp.int32, (1, L), 1)
    sub = lax.broadcasted_iota(jnp.int32, (L, 1), 0)
    lane128 = lax.broadcasted_iota(jnp.int32, (1, 128), 1)

    def prepare_rows(t):
        pltpu.make_async_copy(row_buf.at[t], row_buf.at[t], row_recv.at[t]).wait()
        scale = jnp.zeros((1, 128), f32)
        for g in range(HT):
            scale = jnp.where(lane128 // D == g, temper[t * HT + g] * LOG2E, scale)

        def one(i, _):
            q = row_buf[t, i].astype(f32)
            ok = sub < row_len[i]
            filled = jnp.where(ok, q, q[0:1]) * scale
            hi = filled.astype(bf16).astype(f32)
            lo = filled - hi
            for g in range(HT):
                mine = lane128 // D == g
                ql[i, t * HT + g, :, 0:128] = jnp.where(mine, hi, 0.0).astype(bf16)
                ql[i, t * HT + g, :, 128:256] = jnp.where(mine, lo, 0.0).astype(bf16)
            flat = jnp.where(ok, q, 0.0).T
            ones = jnp.where(lane < row_len[i], 1.0, 0.0)
            pad = jnp.zeros((15, L), f32)
            for g in range(HT):
                own = flat[g * D:(g + 1) * D]
                qf[i, t * HT + g] = own
                qt[i, t * HT + g] = jnp.concatenate([own, ones, pad], axis=0).astype(bf16)
            return 0

        lax.fori_loop(0, R, one, 0)

    def prepare_cols(t):
        pltpu.make_async_copy(col_buf.at[t], col_buf.at[t], col_recv.at[t]).wait()
        o = lax.broadcasted_iota(jnp.int32, (256, 256), 0)
        m = lax.broadcasted_iota(jnp.int32, (256, 256), 1)
        source = lax.rem(o // 4, 16) * 16 + (o // 64) * 4 + lax.rem(o, 4)
        order = jnp.where(m == source, 1.0, 0.0).astype(bf16)
        for g in range(4):
            block = col_buf[t, g * 16:(g + 1) * 16].reshape(256, 128)
            moved = dot(order, block).astype(bf16)
            for j in range(C):
                col_nat[j, g * 64:(g + 1) * 64, :] = moved[j * 64:(j + 1) * 64]
        eye = jnp.where(lax.broadcasted_iota(jnp.int32, (128, 128), 0)
                        == lax.broadcasted_iota(jnp.int32, (128, 128), 1), 1.0, 0.0).astype(bf16)
        pad = jnp.zeros((15, L), f32)
        for j in range(C):
            flat = dot_t(eye, col_nat[j])
            ok = lane < col_len[j]
            filled = jnp.where(ok, flat, flat[:, 0:1]).astype(bf16)
            span = pl.ds((j % 2) * L, L)
            kt[j // 2, t, 0:128, span] = filled
            kt[j // 2, t, 128:256, span] = filled
            flat = jnp.where(ok, flat, 0.0)
            ones = jnp.where(ok, 1.0, 0.0)
            for g in range(HT):
                own = flat[g * D:(g + 1) * D]
                kf[j // 2, t * HT + g, :, span] = own
                vt[j, t * HT + g] = jnp.concatenate([own, ones, pad], axis=0).astype(bf16)

    def place(s):
        s = jnp.maximum(s, 0)
        return s // (2 * R), lax.rem(s // R, 2), lax.rem(s, R)

    def stage_scores(s, g):
        t, jp, i = place(s)
        scores[g] = dot(ql[i, t * HT + g], kt[jp, t])

    def stage_weights(g):
        for u in range(2):
            block = scores[g, :, u * L:(u + 1) * L]
            e_row[g, u] = jnp.exp2(block - jnp.max(block, axis=1, keepdims=True)).astype(bf16)
            e_col[g, :, u * L:(u + 1) * L] = jnp.exp2(block - jnp.max(block, axis=0, keepdims=True)).astype(bf16)

    def readout(product, own, vector):
        term = jnp.tanh(product[:D] * (1.0 / product[D:D + 1]) + own) * vector
        return term[0:8] + term[8:16] + term[16:24] + term[24:32]

    def stage_sums(s, g):
        t, jp, i = place(s)
        h = t * HT + g
        toward_rows = dot(qt[i, h], e_col[g])
        sides = [dot_t(vt[jp * 2 + u, h], e_row[g, u]) for u in range(2)]
        real = s >= 0
        for u in range(2):
            weight = valid[i, jp * 2 + u].astype(f32)
            span = pl.ds(u * L, L)
            row_term = readout(sides[u], qf[i, h], rv[h]) * weight
            col_term = readout(toward_rows[:, u * L:(u + 1) * L], kf[jp, h, :, span], cv[h]) * weight
            row_acc[i] += jnp.where(real, row_term, 0.0)
            col_acc[jp, :, span] += jnp.where(real, col_term, 0.0)

    prepare_rows(0)
    prepare_cols(0)

    def step(s, _):
        @pl.when(s == STEPS // 2)
        def _():
            prepare_rows(1)
            prepare_cols(1)

        for g in range(HT):
            stage_scores(s, g)
            stage_weights((g + 3) % 4)
            stage_sums(s if g >= 2 else s - 1, (g + 2) % 4)
        return 0

    lax.fori_loop(0, STEPS, step, 0)
    stage_weights(3)
    stage_sums(STEPS - 1, 2)
    stage_sums(STEPS - 1, 3)

    row_scale = 1.0 / math.sqrt(C * N_COL)
    col_scale = 1.0 / math.sqrt(R * N_ROW)
    for i in range(R):
        total = jnp.sum(row_acc[i], axis=0, keepdims=True) * row_scale
        total = jnp.where(lane < row_len[i], total, 0.0)
        for t in range(2):
            row_res[t, i:i + 1, :] = total[:, t * 128:(t + 1) * 128]
    row_res[:, R:8, :] = jnp.zeros((2, 8 - R, 128), f32)

    dest = lax.broadcasted_iota(jnp.int32, (N_ROW, L), 0)
    slot = lax.broadcasted_iota(jnp.int32, (N_ROW, L), 1)
    mine = slot // 4 == dest
    from_b = lax.broadcasted_iota(jnp.int32, (L, 128), 0)
    to_lane = lax.broadcasted_iota(jnp.int32, (L, 128), 1)
    msg = jnp.zeros((N_ROW, 128), f32)
    for j in range(C):
        total = jnp.sum(col_acc[j // 2, :, (j % 2) * L:(j % 2 + 1) * L], axis=0, keepdims=True) * col_scale
        total = jnp.where(lane < col_len[j], total, 0.0)
        spread = jnp.where(mine, total, 0.0)
        pick = jnp.where(to_lane == j * 4 + lax.rem(from_b, 4), 1.0, 0.0)
        msg = msg + jnp.dot(spread, pick, precision=lax.Precision.HIGHEST, preferred_element_type=f32)
    col_msg[...] = msg.reshape(N_ROW, 1, 128)

    def send_col_res(k, _):
        to = lax.rem(r + k, N_ROW)
        pltpu.make_async_remote_copy(
            src_ref=col_msg.at[to], dst_ref=col_got.at[r],
            send_sem=cres_send, recv_sem=cres_recv,
            device_id=(to, c), device_id_type=MESH).start()
        return 0

    def send_row_res(k, _):
        to = lax.rem(c + k, N_COL)
        pltpu.make_async_remote_copy(
            src_ref=row_res.at[to // 4], dst_ref=row_got.at[c],
            send_sem=rres_send, recv_sem=rres_recv,
            device_id=(r, to), device_id_type=MESH).start()
        return 0

    lax.fori_loop(1, N_ROW, send_col_res, 0)
    lax.fori_loop(1, N_COL, send_row_res, 0)
    pltpu.make_async_copy(col_msg.at[r], col_got.at[r], cres_recv).start()
    pltpu.make_async_copy(row_res.at[c // 4], row_got.at[c], rres_recv).start()

    pltpu.make_async_copy(row_got, row_got, rres_recv).wait()
    total = row_got[0]
    for k in range(1, N_COL):
        total = total + row_got[k]
    quarter = lax.rem(c, 4)
    answer = total[0:R, 0:32]
    for g in range(1, 4):
        answer = jnp.where(quarter == g, total[0:R, g * 32:(g + 1) * 32], answer)
    row_out[...] = answer

    pltpu.make_async_copy(col_got, col_got, cres_recv).wait()
    total = jnp.sum(col_got[...], axis=0)
    for j in range(C):
        col_out[j:j + 1, :] = total[:, j * 4:(j + 1) * 4]

    for t in range(2):
        others = pl.ds(0, N_ROW - 1)
        pltpu.make_async_copy(col_buf.at[t, others], col_buf.at[t, others], col_send).wait()
        most = pl.ds(0, 32 * (N_COL - 1))
        pltpu.make_async_copy(row_buf.at[t, :, most, :], row_buf.at[t, :, most, :], row_send).wait()
    others = pl.ds(0, N_ROW - 1)
    pltpu.make_async_copy(col_got.at[others], col_got.at[others], cres_send).wait()
    others = pl.ds(0, N_COL - 1)
    pltpu.make_async_copy(row_got.at[others], row_got.at[others], rres_send).wait()


def body(row_embed, col_embed, row_length, col_length, pair_valid, temper, row_vector, col_vector):
    vmem = pl.BlockSpec(memory_space=pltpu.VMEM)
    smem = pl.BlockSpec(memory_space=pltpu.SMEM)
    hbm = pl.BlockSpec(memory_space=pl.ANY)
    dma = pltpu.SemaphoreType.DMA
    return pl.pallas_call(
        kernel,
        out_shape=[jax.ShapeDtypeStruct((R, 32), f32), jax.ShapeDtypeStruct((C, 4), f32)],
        in_specs=[hbm, vmem, smem, smem, smem, smem, vmem, vmem],
        out_specs=[vmem, vmem],
        scratch_shapes=[
            pltpu.VMEM((2, 16, 128), bf16),
            pltpu.VMEM((2, R, L, 128), bf16),
            pltpu.VMEM((2, N_ROW, 16, 128), bf16),
            pltpu.VMEM((C, L, 128), bf16),
            pltpu.VMEM((R, NH, L, 256), bf16),
            pltpu.VMEM((C // 2, 2, 256, 2 * L), bf16),
            pltpu.VMEM((R, NH, 48, L), bf16),
            pltpu.VMEM((C, NH, 48, L), bf16),
            pltpu.VMEM((R, NH, D, L), f32),
            pltpu.VMEM((C // 2, NH, D, 2 * L), f32),
            pltpu.VMEM((NH, D, L), f32),
            pltpu.VMEM((NH, D, L), f32),
            pltpu.VMEM((HT, L, 2 * L), f32),
            pltpu.VMEM((HT, 2, L, L), bf16),
            pltpu.VMEM((HT, L, 2 * L), bf16),
            pltpu.VMEM((R, 8, L), f32),
            pltpu.VMEM((C // 2, 8, 2 * L), f32),
            pltpu.VMEM((2, 8, 128), f32),
            pltpu.VMEM((N_COL, 8, 128), f32),
            pltpu.VMEM((N_ROW, 1, 128), f32),
            pltpu.VMEM((N_ROW, 1, 128), f32),
            dma, dma((2,)), dma, dma((2,)), dma, dma, dma, dma,
        ],
        compiler_params=pltpu.CompilerParams(
            collective_id=0, has_side_effects=True, vmem_limit_bytes=48 * 2**20),
    )(row_embed, col_embed, row_length, col_length, pair_valid, temper,
      row_vector.reshape(1, H), col_vector.reshape(1, H))


def solution(mesh):
    in_specs = (
        P("row", "col", None),
        P("col", "row", None),
        P("row"),
        P("col"),
        P("row", "col"),
        P(),
        P(),
        P(),
    )
    out_specs = (P("row", "col"), P("col", "row"))
    return jax.shard_map(body, mesh=mesh, in_specs=in_specs, out_specs=out_specs, check_vma=False)
```

```python
import functools
import math

import jax
import jax.numpy as jnp
from jax import lax
from jax.experimental import pallas as pl
from jax.experimental.pallas import tpu as pltpu
from jax.sharding import PartitionSpec as P

MESH = pl.DeviceIdType.MESH
f32 = jnp.float32
bf16 = jnp.bfloat16
LOG2E = math.log2(math.e)

N_ROW = 64
N_COL = 8
R = 4
C = 4
L = 256
H = 256
NH = 8
D = H // NH
HT = 128 // D
STEPS = 2 * (C // 2) * R


def dot(a, b):
    return jnp.dot(a, b, preferred_element_type=f32)


def dot_t(a, b):
    return lax.dot_general(a, b, (((1,), (1,)), ((), ())), preferred_element_type=f32)


def kernel(
    row_hbm, col_hbm, row_len_hbm, col_len_hbm, valid_hbm, temper_hbm, row_vec_hbm, col_vec_hbm,
    row_out, col_out,
    col_in, row_len, col_len, valid, temper, row_vec, col_vec,
    row_buf, col_buf, col_nat,
    ql, kt, qt, vt, qf, kf, rv, cv,
    scores, e_row, e_col, row_acc, col_acc,
    row_res, row_got, col_msg, col_got,
    in_sem, far_send, far_recv, near_send, near_recv, row_send, row_recv, twin_send, twin_recv, own_sem,
    rres_send, rres_recv, cres_send, cres_recv,
):
    r = lax.axis_index("row")
    c = lax.axis_index("col")
    z, x, yh = r // 8, lax.rem(r // 2, 4), lax.rem(r, 2)
    yl, core = c // 2, lax.rem(c, 2)
    zh = z // 4

    def device(dz, dx, dyh):
        return (lax.rem(z + dz, 8) * 8 + lax.rem(x + dx, 4) * 2 + lax.rem(yh + dyh, 2), c)

    def near(k, back):
        two = jnp.where((core == 0) != back, 2, 6)
        kz = k // 4
        dz = jnp.where(kz == 3, two, jnp.where(kz == 2, 7, kz))
        dx = lax.rem(k, 4)
        return device(dz, 4 - dx if back else dx, 0)

    def far(k):
        return device((k // 2) * 4, 0, lax.rem(k, 2))

    def along(k):
        return (r, lax.rem(yl + k, 4) * 2 + core)

    twin = (r, yl * 2 + 1 - core)

    small = [(col_hbm, col_in), (row_len_hbm, row_len), (col_len_hbm, col_len), (valid_hbm, valid),
             (temper_hbm, temper), (row_vec_hbm, row_vec), (col_vec_hbm, col_vec)]
    copies = [pltpu.make_async_copy(src, dst, in_sem.at[n]) for n, (src, dst) in enumerate(small)]
    for copy in copies:
        copy.start()
    own_rows = pl.ds(pl.multiple_of(core * 128 + yl * 32, 32), 32)
    own_row_copy = pltpu.make_async_copy(row_hbm, row_buf.at[:, own_rows, :], own_sem)
    own_row_copy.start()

    barrier = pltpu.get_barrier_semaphore()

    def greet(target):
        pl.semaphore_signal(barrier, inc=1, device_id=target, device_id_type=MESH)
        return 0

    lax.fori_loop(1, 4, lambda k, _: greet(far(k)), 0)
    lax.fori_loop(1, 16, lambda k, _: greet(near(k, True)), 0)
    lax.fori_loop(1, 4, lambda k, _: greet(along(k)), 0)
    greet(twin)

    for copy in copies:
        copy.wait()
    block = (lax.rem(z, 4) * 4 + x) * 4
    slot = block + zh * 2 + yh
    own = jnp.concatenate([col_in[j].astype(f32) for j in range(C)], axis=0).astype(bf16)
    for t in range(2):
        col_buf[t, slot] = own[:, t * 128:(t + 1) * 128]

    pl.semaphore_wait(barrier, 22)

    def send_far(k, _):
        pltpu.make_async_remote_copy(
            src_ref=col_buf.at[:, slot], dst_ref=col_buf.at[:, slot],
            send_sem=far_send, recv_sem=far_recv.at[k - 1],
            device_id=far(k), device_id_type=MESH).start()
        return 0

    lax.fori_loop(1, 4, send_far, 0)

    def send_rows(t):
        half = pl.ds(t * 128, 128)

        def one(k, _):
            pltpu.make_async_remote_copy(
                src_ref=row_hbm.at[:, :, half], dst_ref=row_buf.at[:, own_rows, half],
                send_sem=row_send, recv_sem=row_recv.at[t],
                device_id=along(k), device_id_type=MESH).start()
            return 0

        lax.fori_loop(1, 4, one, 0)

    def send_near(t, part):
        pair = pl.ds(block + part * 2, 2)

        def one(k, _):
            pltpu.make_async_remote_copy(
                src_ref=col_buf.at[t, pair], dst_ref=col_buf.at[t, pair],
                send_sem=near_send, recv_sem=near_recv.at[t],
                device_id=near(k, False), device_id_type=MESH).start()
            return 0

        lax.fori_loop(1, 16, one, 0)

    same_core = pl.ds(pl.multiple_of(core * 128, 128), 128)

    def pass_rows(t):
        half = pl.ds(t * 128, 128)
        three = row_buf.at[:, pl.ds(0, 96), half]
        pltpu.make_async_copy(three, three, row_recv.at[t]).wait()
        pltpu.make_async_remote_copy(
            src_ref=row_buf.at[:, same_core, half], dst_ref=row_buf.at[:, same_core, half],
            send_sem=twin_send, recv_sem=twin_recv.at[t],
            device_id=twin, device_id_type=MESH).start()

    def await_far(k):
        pltpu.make_async_copy(col_buf.at[:, 0], col_buf.at[:, 0], far_recv.at[k - 1]).wait()

    send_rows(0)
    send_rows(1)
    await_far(1)
    send_near(0, zh)
    await_far(2)
    await_far(3)
    send_near(0, 1 - zh)
    own_row_copy.wait()
    pass_rows(0)
    send_near(1, zh)
    send_near(1, 1 - zh)
    pass_rows(1)

    rv[...] = jnp.broadcast_to(row_vec[...], (L, H)).T.reshape(NH, D, L)
    cv[...] = jnp.broadcast_to(col_vec[...], (L, H)).T.reshape(NH, D, L)
    row_acc[...] = jnp.zeros_like(row_acc)
    col_acc[...] = jnp.zeros_like(col_acc)

    def row_residue(place):
        return (lax.rem(place // 32, 4) * 2 + place // 128) * 32 + lax.rem(place, 32)

    def col_residue(place):
        s = place // 4
        device_z = s // 16 + lax.rem(s // 2, 2) * 4
        return ((device_z * 4 + lax.rem(s // 4, 4)) * 2 + lax.rem(s, 2)) * 4 + lax.rem(place, 4)

    lane = lax.broadcasted_iota(jnp.int32, (1, L), 1)
    row_lane, col_lane = row_residue(lane), col_residue(lane)
    row_sub = row_residue(lax.broadcasted_iota(jnp.int32, (L, 1), 0))
    lane128 = lax.broadcasted_iota(jnp.int32, (1, 128), 1)

    def prepare_rows(t):
        half = pl.ds(t * 128, 128)
        theirs = row_buf.at[:, pl.ds(0, 128), half]
        pltpu.make_async_copy(theirs, theirs, twin_recv.at[t]).wait()
        scale = jnp.zeros((1, 128), f32)
        for g in range(HT):
            scale = jnp.where(lane128 // D == g, temper[t * HT + g] * LOG2E, scale)

        def one(i, _):
            q = row_buf[i, :, half].astype(f32)
            ok = row_sub < row_len[i]
            filled = jnp.where(ok, q, q[0:1]) * scale
            hi = filled.astype(bf16).astype(f32)
            lo = filled - hi
            for g in range(HT):
                mine = lane128 // D == g
                ql[i, t * HT + g, :, 0:128] = jnp.where(mine, hi, 0.0).astype(bf16)
                ql[i, t * HT + g, :, 128:256] = jnp.where(mine, lo, 0.0).astype(bf16)
            flat = jnp.where(ok, q, 0.0).T
            ones = jnp.where(row_lane < row_len[i], 1.0, 0.0)
            pad = jnp.zeros((15, L), f32)
            for g in range(HT):
                own = flat[g * D:(g + 1) * D]
                qf[i, t * HT + g] = own
                qt[i, t * HT + g] = jnp.concatenate([own, ones, pad], axis=0).astype(bf16)
            return 0

        lax.fori_loop(0, R, one, 0)

    def prepare_cols(t):
        theirs = col_buf.at[t, pl.ds(0, 60)]
        pltpu.make_async_copy(theirs, theirs, near_recv.at[t]).wait()
        o = lax.broadcasted_iota(jnp.int32, (256, 256), 0)
        m = lax.broadcasted_iota(jnp.int32, (256, 256), 1)
        source = lax.rem(o // 4, 16) * 16 + (o // 64) * 4 + lax.rem(o, 4)
        order = jnp.where(m == source, 1.0, 0.0).astype(bf16)
        for g in range(4):
            block = col_buf[t, g * 16:(g + 1) * 16].reshape(256, 128)
            moved = dot(order, block).astype(bf16)
            for j in range(C):
                col_nat[j, g * 64:(g + 1) * 64, :] = moved[j * 64:(j + 1) * 64]
        eye = jnp.where(lax.broadcasted_iota(jnp.int32, (128, 128), 0)
                        == lax.broadcasted_iota(jnp.int32, (128, 128), 1), 1.0, 0.0).astype(bf16)
        pad = jnp.zeros((15, L), f32)
        for j in range(C):
            flat = dot_t(eye, col_nat[j])
            ok = col_lane < col_len[j]
            filled = jnp.where(ok, flat, flat[:, 0:1]).astype(bf16)
            span = pl.ds((j % 2) * L, L)
            kt[j // 2, t, 0:128, span] = filled
            kt[j // 2, t, 128:256, span] = filled
            flat = jnp.where(ok, flat, 0.0)
            ones = jnp.where(ok, 1.0, 0.0)
            for g in range(HT):
                own = flat[g * D:(g + 1) * D]
                kf[j // 2, t * HT + g, :, span] = own
                vt[j, t * HT + g] = jnp.concatenate([own, ones, pad], axis=0).astype(bf16)

    def place(s):
        s = jnp.maximum(s, 0)
        return s // (2 * R), lax.rem(s // R, 2), lax.rem(s, R)

    def stage_scores(s, g):
        t, jp, i = place(s)
        scores[g] = dot(ql[i, t * HT + g], kt[jp, t])

    def stage_weights(g):
        for u in range(2):
            block = scores[g, :, u * L:(u + 1) * L]
            e_row[g, u] = jnp.exp2(block - jnp.max(block, axis=1, keepdims=True)).astype(bf16)
            e_col[g, :, u * L:(u + 1) * L] = jnp.exp2(block - jnp.max(block, axis=0, keepdims=True)).astype(bf16)

    def readout(product, own, vector):
        term = jnp.tanh(product[:D] * (1.0 / product[D:D + 1]) + own) * vector
        return term[0:8] + term[8:16] + term[16:24] + term[24:32]

    def stage_sums(s, g):
        t, jp, i = place(s)
        h = t * HT + g
        toward_rows = dot(qt[i, h], e_col[g])
        sides = [dot_t(vt[jp * 2 + u, h], e_row[g, u]) for u in range(2)]
        real = s >= 0
        for u in range(2):
            weight = valid[i, jp * 2 + u].astype(f32)
            span = pl.ds(u * L, L)
            row_term = readout(sides[u], qf[i, h], rv[h]) * weight
            col_term = readout(toward_rows[:, u * L:(u + 1) * L], kf[jp, h, :, span], cv[h]) * weight
            row_acc[i] += jnp.where(real, row_term, 0.0)
            col_acc[jp, :, span] += jnp.where(real, col_term, 0.0)

    prepare_rows(0)
    prepare_cols(0)

    def step(s, _):
        @pl.when(s == STEPS // 2)
        def _():
            prepare_rows(1)
            prepare_cols(1)

        for g in range(HT):
            stage_scores(s, g)
            stage_weights((g + 3) % 4)
            stage_sums(s if g >= 2 else s - 1, (g + 2) % 4)
        return 0

    lax.fori_loop(0, STEPS, step, 0)
    stage_weights(3)
    stage_sums(STEPS - 1, 2)
    stage_sums(STEPS - 1, 3)

    row_scale = 1.0 / math.sqrt(C * N_COL)
    col_scale = 1.0 / math.sqrt(R * N_ROW)
    for i in range(R):
        total = jnp.sum(row_acc[i], axis=0, keepdims=True) * row_scale
        total = jnp.where(row_lane < row_len[i], total, 0.0)
        for t in range(2):
            row_res[t, i:i + 1, :] = total[:, t * 128:(t + 1) * 128]
    row_res[:, R:8, :] = jnp.zeros((2, 8 - R, 128), f32)

    dest = lax.broadcasted_iota(jnp.int32, (N_ROW, L), 0)
    mine = lax.broadcasted_iota(jnp.int32, (N_ROW, L), 1) // 4 == dest
    from_b = lax.broadcasted_iota(jnp.int32, (L, 128), 0)
    to_lane = lax.broadcasted_iota(jnp.int32, (L, 128), 1)
    msg = jnp.zeros((N_ROW, 128), f32)
    for j in range(C):
        total = jnp.sum(col_acc[j // 2, :, (j % 2) * L:(j % 2 + 1) * L], axis=0, keepdims=True) * col_scale
        total = jnp.where(col_lane < col_len[j], total, 0.0)
        spread = jnp.where(mine, total, 0.0)
        pick = jnp.where(to_lane == j * 4 + lax.rem(from_b, 4), 1.0, 0.0)
        msg = msg + jnp.dot(spread, pick, precision=lax.Precision.HIGHEST, preferred_element_type=f32)
    col_msg[...] = msg.reshape(N_ROW, 1, 128)

    def send_col_res(k, _):
        n, m = k // 8, lax.rem(k, 8)
        dz = lax.rem(12 + jnp.where(lax.rem(n, 2) == 1, -((n + 1) // 2), n // 2), 8)
        dx, dyh = lax.rem(m // 2 + 2, 4), lax.rem(m + 1, 2)
        to_z, to_x, to_yh = lax.rem(z + dz, 8), lax.rem(x + dx, 4), lax.rem(yh + dyh, 2)
        place = (lax.rem(to_z, 4) * 4 + to_x) * 4 + (to_z // 4) * 2 + to_yh
        pltpu.make_async_remote_copy(
            src_ref=col_msg.at[place], dst_ref=col_got.at[r],
            send_sem=cres_send, recv_sem=cres_recv,
            device_id=device(dz, dx, dyh), device_id_type=MESH).start()
        return 0

    def send_row_res(k, _):
        to = lax.rem(c + k, N_COL)
        pltpu.make_async_remote_copy(
            src_ref=row_res.at[lax.rem(to, 2)], dst_ref=row_got.at[c],
            send_sem=rres_send, recv_sem=rres_recv,
            device_id=(r, to), device_id_type=MESH).start()
        return 0

    lax.fori_loop(0, 61, send_col_res, 0)
    lax.fori_loop(62, 64, send_col_res, 0)
    lax.fori_loop(1, N_COL, send_row_res, 0)
    pltpu.make_async_copy(col_msg.at[slot], col_got.at[r], cres_recv).start()
    pltpu.make_async_copy(row_res.at[core], row_got.at[c], rres_recv).start()

    pltpu.make_async_copy(row_got, row_got, rres_recv).wait()
    total = row_got[0]
    for k in range(1, N_COL):
        total = total + row_got[k]
    quarter = yl
    answer = total[0:R, 0:32]
    for g in range(1, 4):
        answer = jnp.where(quarter == g, total[0:R, g * 32:(g + 1) * 32], answer)
    row_out[...] = answer

    pltpu.make_async_copy(col_got, col_got, cres_recv).wait()
    total = jnp.sum(col_got[...], axis=0)
    for j in range(C):
        col_out[j:j + 1, :] = total[:, j * 4:(j + 1) * 4]

    three = col_buf.at[:, pl.ds(0, 3)]
    pltpu.make_async_copy(three, three, far_send).wait()
    for t in range(2):
        sixty = col_buf.at[t, pl.ds(0, 60)]
        pltpu.make_async_copy(sixty, sixty, near_send).wait()
    most = row_buf.at[:, pl.ds(0, 96), :]
    pltpu.make_async_copy(most, most, row_send).wait()
    most = row_buf.at[:, pl.ds(0, 128), :]
    pltpu.make_async_copy(most, most, twin_send).wait()
    others = pl.ds(0, N_ROW - 1)
    pltpu.make_async_copy(col_got.at[others], col_got.at[others], cres_send).wait()
    others = pl.ds(0, N_COL - 1)
    pltpu.make_async_copy(row_got.at[others], row_got.at[others], rres_send).wait()


def body(row_embed, col_embed, row_length, col_length, pair_valid, temper, row_vector, col_vector):
    vmem = pl.BlockSpec(memory_space=pltpu.VMEM)
    hbm = pl.BlockSpec(memory_space=pltpu.HBM)
    dma = pltpu.SemaphoreType.DMA
    return pl.pallas_call(
        kernel,
        out_shape=[jax.ShapeDtypeStruct((R, 32), f32), jax.ShapeDtypeStruct((C, 4), f32)],
        in_specs=[hbm] * 8,
        out_specs=[vmem, vmem],
        scratch_shapes=[
            pltpu.VMEM((C, 4, H), bf16),
            pltpu.SMEM((R,), jnp.int32),
            pltpu.SMEM((C,), jnp.int32),
            pltpu.SMEM((R, C), jnp.int32),
            pltpu.SMEM((NH,), f32),
            pltpu.VMEM((1, H), f32),
            pltpu.VMEM((1, H), f32),
            pltpu.VMEM((R, L, H), bf16),
            pltpu.VMEM((2, N_ROW, 16, 128), bf16),
            pltpu.VMEM((C, L, 128), bf16),
            pltpu.VMEM((R, NH, L, 256), bf16),
            pltpu.VMEM((C // 2, 2, 256, 2 * L), bf16),
            pltpu.VMEM((R, NH, 48, L), bf16),
            pltpu.VMEM((C, NH, 48, L), bf16),
            pltpu.VMEM((R, NH, D, L), f32),
            pltpu.VMEM((C // 2, NH, D, 2 * L), f32),
            pltpu.VMEM((NH, D, L), f32),
            pltpu.VMEM((NH, D, L), f32),
            pltpu.VMEM((HT, L, 2 * L), f32),
            pltpu.VMEM((HT, 2, L, L), bf16),
            pltpu.VMEM((HT, L, 2 * L), bf16),
            pltpu.VMEM((R, 8, L), f32),
            pltpu.VMEM((C // 2, 8, 2 * L), f32),
            pltpu.VMEM((2, 8, 128), f32),
            pltpu.VMEM((N_COL, 8, 128), f32),
            pltpu.VMEM((N_ROW, 1, 128), f32),
            pltpu.VMEM((N_ROW, 1, 128), f32),
            dma((7,)), dma, dma((3,)), dma, dma((2,)), dma, dma((2,)), dma, dma((2,)), dma,
            dma, dma, dma, dma,
        ],
        compiler_params=pltpu.CompilerParams(
            collective_id=0, has_side_effects=True, vmem_limit_bytes=64 * 2**20),
    )(row_embed, col_embed, row_length, col_length, pair_valid, temper,
      row_vector.reshape(1, H), col_vector.reshape(1, H))


def solution(mesh):
    in_specs = (
        P("row", "col", None),
        P("col", "row", None),
        P("row"),
        P("col"),
        P("row", "col"),
        P(),
        P(),
        P(),
    )
    out_specs = (P("row", "col"), P("col", "row"))
    return jax.shard_map(body, mesh=mesh, in_specs=in_specs, out_specs=out_specs, check_vma=False)
```

```python
import functools
import math

import jax
import jax.numpy as jnp
from jax import lax
from jax.experimental import pallas as pl
from jax.experimental.pallas import tpu as pltpu
from jax.sharding import PartitionSpec as P

MESH = pl.DeviceIdType.MESH
f32 = jnp.float32
bf16 = jnp.bfloat16
LOG2E = math.log2(math.e)

N_ROW = 64
N_COL = 8
R = 4
C = 4
L = 256
H = 256
NH = 8
D = H // NH
HT = 128 // D
STEPS = 2 * (C // 2) * R
UNROLL = 4


def dot(a, b):
    return jnp.dot(a, b, preferred_element_type=f32)


def dot_t(a, b):
    return lax.dot_general(a, b, (((1,), (1,)), ((), ())), preferred_element_type=f32)


def kernel(
    row_hbm, col_hbm, row_len_hbm, col_len_hbm, valid_hbm, temper_hbm, row_vec_hbm, col_vec_hbm,
    out,
    col_in, row_len, col_len, valid, temper, row_vec, col_vec,
    row_buf, col_buf, col_nat,
    ql, kt, qt, vt, qf, kf, rv, cv,
    scores, e_row, e_col, row_acc, col_acc,
    row_res, row_got, col_msg, col_got,
    in_sem, far_send, far_recv, near_send, near_recv, row_send, row_recv, twin_send, twin_recv, own_sem,
    rres_send, rres_recv, cres_send, cres_recv,
):
    r = lax.axis_index("row")
    c = lax.axis_index("col")
    z, x, yh = r // 8, lax.rem(r // 2, 4), lax.rem(r, 2)
    yl, core = c // 2, lax.rem(c, 2)
    zh = z // 4

    def device(dz, dx, dyh):
        return (lax.rem(z + dz, 8) * 8 + lax.rem(x + dx, 4) * 2 + lax.rem(yh + dyh, 2), c)

    def near(k, back):
        kz = k // 4
        dz = jnp.where(kz == 3, jnp.where((core == 0) != back, 2, 6), jnp.where(kz == 2, 7, kz))
        dx = lax.rem(k, 4)
        return device(dz, 4 - dx if back else dx, 0)

    other_y, other_z = device(0, 0, 1), device(4, 0, 0)

    def along(k):
        return (r, lax.rem(yl + k, 4) * 2 + core)

    twin = (r, yl * 2 + 1 - core)

    small = [(col_hbm, col_in), (row_len_hbm, row_len), (col_len_hbm, col_len), (valid_hbm, valid),
             (temper_hbm, temper), (row_vec_hbm, row_vec), (col_vec_hbm, col_vec)]
    copies = [pltpu.make_async_copy(src, dst, in_sem.at[n]) for n, (src, dst) in enumerate(small)]
    for copy in copies:
        copy.start()
    own_rows = pl.ds(pl.multiple_of(core * 128 + yl * 32, 32), 32)
    own_row_copy = pltpu.make_async_copy(row_hbm, row_buf.at[:, own_rows, :], own_sem)
    own_row_copy.start()

    barrier = pltpu.get_barrier_semaphore()

    def greet(target):
        pl.semaphore_signal(barrier, inc=1, device_id=target, device_id_type=MESH)
        return 0

    greet(other_y)
    greet(other_z)
    lax.fori_loop(1, 16, lambda k, _: greet(near(k, True)), 0)
    lax.fori_loop(1, 4, lambda k, _: greet(along(k)), 0)
    greet(twin)

    for copy in copies:
        copy.wait()
    block = (lax.rem(z, 4) * 4 + x) * 4
    slot = block + zh * 2 + yh
    col_buf[slot] = jnp.concatenate([col_in[j].astype(f32) for j in range(C)], axis=0).astype(bf16)

    pl.semaphore_wait(barrier, 21)

    def send_far(span, n, target):
        pltpu.make_async_remote_copy(
            src_ref=col_buf.at[span], dst_ref=col_buf.at[span],
            send_sem=far_send.at[n], recv_sem=far_recv.at[n],
            device_id=target, device_id_type=MESH).start()

    send_far(pl.ds(slot, 1), 0, other_y)

    def send_rows(t):
        half = pl.ds(t * 128, 128)

        def one(k, _):
            pltpu.make_async_remote_copy(
                src_ref=row_hbm.at[:, :, half], dst_ref=row_buf.at[:, own_rows, half],
                send_sem=row_send, recv_sem=row_recv.at[t],
                device_id=along(k), device_id_type=MESH).start()
            return 0

        lax.fori_loop(1, 4, one, 0)

    def send_near(part):
        pair = pl.ds(block + part * 2, 2)

        def one(k, _):
            pltpu.make_async_remote_copy(
                src_ref=col_buf.at[pair], dst_ref=col_buf.at[pair],
                send_sem=near_send, recv_sem=near_recv,
                device_id=near(k, False), device_id_type=MESH).start()
            return 0

        lax.fori_loop(1, 16, one, 0)

    def await_far(n):
        theirs = col_buf.at[pl.ds(0, n + 1)]
        pltpu.make_async_copy(theirs, theirs, far_recv.at[n]).wait()

    same_core = pl.ds(pl.multiple_of(core * 128, 128), 128)

    def pass_rows(t):
        half = pl.ds(t * 128, 128)
        three = row_buf.at[:, pl.ds(0, 96), half]
        pltpu.make_async_copy(three, three, row_recv.at[t]).wait()
        pltpu.make_async_remote_copy(
            src_ref=row_buf.at[:, same_core, half], dst_ref=row_buf.at[:, same_core, half],
            send_sem=twin_send, recv_sem=twin_recv.at[t],
            device_id=twin, device_id_type=MESH).start()

    send_rows(0)
    send_rows(1)
    await_far(0)
    send_far(pl.ds(block + zh * 2, 2), 1, other_z)
    send_near(zh)
    own_row_copy.wait()
    pass_rows(0)
    await_far(1)
    send_near(1 - zh)
    pass_rows(1)

    rv[...] = jnp.broadcast_to(row_vec[...], (L, H)).T.reshape(NH, D, L)
    cv[...] = jnp.broadcast_to(col_vec[...], (L, H)).T.reshape(NH, D, L)
    row_acc[...] = jnp.zeros_like(row_acc)
    col_acc[...] = jnp.zeros_like(col_acc)

    def row_residue(place):
        return (lax.rem(place // 32, 4) * 2 + place // 128) * 32 + lax.rem(place, 32)

    def col_residue(place):
        s = place // 4
        device_z = s // 16 + lax.rem(s // 2, 2) * 4
        return ((device_z * 4 + lax.rem(s // 4, 4)) * 2 + lax.rem(s, 2)) * 4 + lax.rem(place, 4)

    lane = lax.broadcasted_iota(jnp.int32, (1, L), 1)
    row_lane, col_lane = row_residue(lane), col_residue(lane)
    row_sub = row_residue(lax.broadcasted_iota(jnp.int32, (L, 1), 0))
    lane128 = lax.broadcasted_iota(jnp.int32, (1, 128), 1)

    def prepare_rows(t):
        half = pl.ds(t * 128, 128)
        theirs = row_buf.at[:, pl.ds(0, 128), half]
        pltpu.make_async_copy(theirs, theirs, twin_recv.at[t]).wait()
        scale = jnp.zeros((1, 128), f32)
        for g in range(HT):
            scale = jnp.where(lane128 // D == g, temper[t * HT + g] * LOG2E, scale)

        def one(i, _):
            q = row_buf[i, :, half].astype(f32)
            ok = row_sub < row_len[i]
            filled = jnp.where(ok, q, q[0:1]) * scale
            hi = filled.astype(bf16).astype(f32)
            lo = filled - hi
            for g in range(HT):
                mine = lane128 // D == g
                ql[i, t * HT + g, :, 0:128] = jnp.where(mine, hi, 0.0).astype(bf16)
                ql[i, t * HT + g, :, 128:256] = jnp.where(mine, lo, 0.0).astype(bf16)
            flat = jnp.where(ok, q, 0.0).T
            ones = jnp.where(row_lane < row_len[i], 1.0, 0.0)
            pad = jnp.zeros((15, L), f32)
            for g in range(HT):
                own = flat[g * D:(g + 1) * D]
                qf[i, t * HT + g] = own
                qt[i, t * HT + g] = jnp.concatenate([own, ones, pad], axis=0).astype(bf16)
            return 0

        lax.fori_loop(0, R, one, 0)

    def prepare_cols(t):
        o = lax.broadcasted_iota(jnp.int32, (256, 256), 0)
        m = lax.broadcasted_iota(jnp.int32, (256, 256), 1)
        source = lax.rem(o // 4, 16) * 16 + (o // 64) * 4 + lax.rem(o, 4)
        order = jnp.where(m == source, 1.0, 0.0).astype(bf16)
        for g in range(4):
            piece = col_buf[g * 16:(g + 1) * 16, :, t * 128:(t + 1) * 128].reshape(256, 128)
            moved = dot(order, piece).astype(bf16)
            for j in range(C):
                col_nat[j, g * 64:(g + 1) * 64, :] = moved[j * 64:(j + 1) * 64]
        eye = jnp.where(lax.broadcasted_iota(jnp.int32, (128, 128), 0)
                        == lax.broadcasted_iota(jnp.int32, (128, 128), 1), 1.0, 0.0).astype(bf16)
        pad = jnp.zeros((15, L), f32)
        for j in range(C):
            flat = dot_t(eye, col_nat[j])
            ok = col_lane < col_len[j]
            filled = jnp.where(ok, flat, flat[:, 0:1]).astype(bf16)
            span = pl.ds((j % 2) * L, L)
            kt[j // 2, t, 0:128, span] = filled
            kt[j // 2, t, 128:256, span] = filled
            flat = jnp.where(ok, flat, 0.0)
            ones = jnp.where(ok, 1.0, 0.0)
            for g in range(HT):
                own = flat[g * D:(g + 1) * D]
                kf[j // 2, t * HT + g, :, span] = own
                vt[j, t * HT + g] = jnp.concatenate([own, ones, pad], axis=0).astype(bf16)

    def place(s):
        s = jnp.maximum(s, 0)
        return s // (2 * R), lax.rem(s // R, 2), lax.rem(s, R)

    def stage_scores(s, g):
        t, jp, i = place(s)
        scores[g] = dot(ql[i, t * HT + g], kt[jp, t])

    def stage_weights(g):
        for u in range(2):
            block = scores[g, :, u * L:(u + 1) * L]
            e_row[g, u] = jnp.exp2(block - jnp.max(block, axis=1, keepdims=True)).astype(bf16)
            e_col[g, :, u * L:(u + 1) * L] = jnp.exp2(block - jnp.max(block, axis=0, keepdims=True)).astype(bf16)

    def readout(product, own, vector):
        term = jnp.tanh(product[:D] * (1.0 / product[D:D + 1]) + own) * vector
        return term[0:8] + term[8:16] + term[16:24] + term[24:32]

    def stage_sums(s, g):
        t, jp, i = place(s)
        h = t * HT + g
        toward_rows = dot(qt[i, h], e_col[g])
        sides = [dot_t(vt[jp * 2 + u, h], e_row[g, u]) for u in range(2)]
        real = s >= 0
        for u in range(2):
            weight = valid[i, jp * 2 + u].astype(f32)
            span = pl.ds(u * L, L)
            row_term = readout(sides[u], qf[i, h], rv[h]) * weight
            col_term = readout(toward_rows[:, u * L:(u + 1) * L], kf[jp, h, :, span], cv[h]) * weight
            row_acc[i] += jnp.where(real, row_term, 0.0)
            col_acc[jp, :, span] += jnp.where(real, col_term, 0.0)

    prepare_rows(0)
    prepare_rows(1)
    theirs = col_buf.at[pl.ds(0, 60)]
    pltpu.make_async_copy(theirs, theirs, near_recv).wait()
    prepare_cols(0)

    def steps(n, _):
        @pl.when(n == STEPS // UNROLL // 2)
        def _():
            prepare_cols(1)

        for i in range(UNROLL):
            s = n * UNROLL + i
            for g in range(HT):
                stage_scores(s, g)
                stage_weights((g + 3) % 4)
                stage_sums(s if g >= 2 else s - 1, (g + 2) % 4)
        return 0

    lax.fori_loop(0, STEPS // UNROLL, steps, 0)
    stage_weights(3)
    stage_sums(STEPS - 1, 2)
    stage_sums(STEPS - 1, 3)

    row_scale = 1.0 / math.sqrt(C * N_COL)
    col_scale = 1.0 / math.sqrt(R * N_ROW)
    for i in range(R):
        total = jnp.sum(row_acc[i], axis=0, keepdims=True) * row_scale
        total = jnp.where(row_lane < row_len[i], total, 0.0)
        for t in range(2):
            row_res[t, i:i + 1, :] = total[:, t * 128:(t + 1) * 128]
    row_res[:, R:8, :] = jnp.zeros((2, 8 - R, 128), f32)

    dest = lax.broadcasted_iota(jnp.int32, (N_ROW, L), 0)
    mine = lax.broadcasted_iota(jnp.int32, (N_ROW, L), 1) // 4 == dest
    from_b = lax.broadcasted_iota(jnp.int32, (3 * L, 128), 0)
    to_lane = lax.broadcasted_iota(jnp.int32, (3 * L, 128), 1)
    pick = jnp.where(to_lane == lax.rem(from_b, 4), 1.0, 0.0).astype(bf16)
    spread = []
    for j in range(C):
        total = jnp.sum(col_acc[j // 2, :, (j % 2) * L:(j % 2 + 1) * L], axis=0, keepdims=True) * col_scale
        total = jnp.where(col_lane < col_len[j], total, 0.0)
        parts = []
        for _ in range(3):
            parts.append(total.astype(bf16).astype(f32))
            total = total - parts[-1]
        spread.append(jnp.concatenate([jnp.where(mine, part, 0.0).astype(bf16) for part in parts], axis=1))
    picked = dot(jnp.concatenate(spread, axis=0), pick)
    msg = picked[0:N_ROW]
    for j in range(1, C):
        msg = msg + pltpu.roll(picked[j * N_ROW:(j + 1) * N_ROW], 4 * j, 1)
    col_msg[...] = msg.reshape(N_ROW, 1, 128)

    def send_col_res(k, _):
        n, m = k // 8, lax.rem(k, 8)
        dz = lax.rem(12 + jnp.where(lax.rem(n, 2) == 1, -((n + 1) // 2), n // 2), 8)
        dx, dyh = lax.rem(m // 2 + 2, 4), lax.rem(m + 1, 2)
        to_z, to_x, to_yh = lax.rem(z + dz, 8), lax.rem(x + dx, 4), lax.rem(yh + dyh, 2)
        place = (lax.rem(to_z, 4) * 4 + to_x) * 4 + (to_z // 4) * 2 + to_yh
        pltpu.make_async_remote_copy(
            src_ref=col_msg.at[place], dst_ref=col_got.at[r],
            send_sem=cres_send, recv_sem=cres_recv,
            device_id=device(dz, dx, dyh), device_id_type=MESH).start()
        return 0

    def send_row_res(k, _):
        to = lax.rem(c + k, N_COL)
        pltpu.make_async_remote_copy(
            src_ref=row_res.at[lax.rem(to, 2)], dst_ref=row_got.at[c],
            send_sem=rres_send, recv_sem=rres_recv,
            device_id=(r, to), device_id_type=MESH).start()
        return 0

    lax.fori_loop(0, 61, send_col_res, 0)
    lax.fori_loop(62, 64, send_col_res, 0)
    lax.fori_loop(1, N_COL, send_row_res, 0)
    pltpu.make_async_copy(col_msg.at[slot], col_got.at[r], cres_recv).start()
    pltpu.make_async_copy(row_res.at[core], row_got.at[c], rres_recv).start()

    pltpu.make_async_copy(row_got, row_got, rres_recv).wait()
    total = row_got[0]
    for k in range(1, N_COL):
        total = total + row_got[k]
    quarter = yl
    answer = total[0:R, 0:32]
    for g in range(1, 4):
        answer = jnp.where(quarter == g, total[0:R, g * 32:(g + 1) * 32], answer)
    out[0:R, 0:32] = answer

    pltpu.make_async_copy(col_got, col_got, cres_recv).wait()
    total = jnp.sum(col_got[...], axis=0)
    for j in range(C):
        out[R + j:R + j + 1, 0:4] = total[:, j * 4:(j + 1) * 4]

    for n in range(2):
        sent = col_buf.at[pl.ds(0, n + 1)]
        pltpu.make_async_copy(sent, sent, far_send.at[n]).wait()
    sent = col_buf.at[pl.ds(0, 60)]
    pltpu.make_async_copy(sent, sent, near_send).wait()
    most = row_buf.at[:, pl.ds(0, 96), :]
    pltpu.make_async_copy(most, most, row_send).wait()
    most = row_buf.at[:, pl.ds(0, 128), :]
    pltpu.make_async_copy(most, most, twin_send).wait()
    others = pl.ds(0, N_ROW - 1)
    pltpu.make_async_copy(col_got.at[others], col_got.at[others], cres_send).wait()
    others = pl.ds(0, N_COL - 1)
    pltpu.make_async_copy(row_got.at[others], row_got.at[others], rres_send).wait()


def body(row_embed, col_embed, row_length, col_length, pair_valid, temper, row_vector, col_vector):
    vmem = pl.BlockSpec(memory_space=pltpu.VMEM)
    hbm = pl.BlockSpec(memory_space=pltpu.HBM)
    dma = pltpu.SemaphoreType.DMA
    result = pl.pallas_call(
        kernel,
        out_shape=jax.ShapeDtypeStruct((R + C, 128), f32),
        in_specs=[hbm] * 8,
        out_specs=vmem,
        scratch_shapes=[
            pltpu.VMEM((C, 4, H), bf16),
            pltpu.SMEM((R,), jnp.int32),
            pltpu.SMEM((C,), jnp.int32),
            pltpu.SMEM((R, C), jnp.int32),
            pltpu.SMEM((NH,), f32),
            pltpu.VMEM((1, H), f32),
            pltpu.VMEM((1, H), f32),
            pltpu.VMEM((R, L, H), bf16),
            pltpu.VMEM((N_ROW, 16, H), bf16),
            pltpu.VMEM((C, L, 128), bf16),
            pltpu.VMEM((R, NH, L, 256), bf16),
            pltpu.VMEM((C // 2, 2, 256, 2 * L), bf16),
            pltpu.VMEM((R, NH, 48, L), bf16),
            pltpu.VMEM((C, NH, 48, L), bf16),
            pltpu.VMEM((R, NH, D, L), f32),
            pltpu.VMEM((C // 2, NH, D, 2 * L), f32),
            pltpu.VMEM((NH, D, L), f32),
            pltpu.VMEM((NH, D, L), f32),
            pltpu.VMEM((HT, L, 2 * L), f32),
            pltpu.VMEM((HT, 2, L, L), bf16),
            pltpu.VMEM((HT, L, 2 * L), bf16),
            pltpu.VMEM((R, 8, L), f32),
            pltpu.VMEM((C // 2, 8, 2 * L), f32),
            pltpu.VMEM((2, 8, 128), f32),
            pltpu.VMEM((N_COL, 8, 128), f32),
            pltpu.VMEM((N_ROW, 1, 128), f32),
            pltpu.VMEM((N_ROW, 1, 128), f32),
            dma((7,)), dma((2,)), dma((2,)), dma, dma, dma, dma((2,)), dma, dma((2,)), dma,
            dma, dma, dma, dma,
        ],
        compiler_params=pltpu.CompilerParams(
            collective_id=0, has_side_effects=True, vmem_limit_bytes=64 * 2**20),
    )(row_embed, col_embed, row_length, col_length, pair_valid, temper,
      row_vector.reshape(1, H), col_vector.reshape(1, H))
    return result[:R, :32], result[R:, :4]


def solution(mesh):
    in_specs = (
        P("row", "col", None),
        P("col", "row", None),
        P("row"),
        P("col"),
        P("row", "col"),
        P(),
        P(),
        P(),
    )
    out_specs = (P("row", "col"), P("col", "row"))
    return jax.shard_map(body, mesh=mesh, in_specs=in_specs, out_specs=out_specs, check_vma=False)
```

```python
import functools
import math

import jax
import jax.numpy as jnp
from jax import lax
from jax.experimental import pallas as pl
from jax.experimental.pallas import tpu as pltpu
from jax.sharding import PartitionSpec as P

MESH = pl.DeviceIdType.MESH
f32 = jnp.float32
bf16 = jnp.bfloat16
LOG2E = math.log2(math.e)

N_ROW = 64
N_COL = 8
R = 4
C = 4
L = 256
H = 256
NH = 8
D = H // NH
HT = 128 // D
STEPS = 2 * (C // 2) * R
UNROLL = 4


def dot(a, b):
    return jnp.dot(a, b, preferred_element_type=f32)


def dot_t(a, b):
    return lax.dot_general(a, b, (((1,), (1,)), ((), ())), preferred_element_type=f32)


def kernel(
    row_hbm, col_hbm, row_len_hbm, col_len_hbm, valid_hbm, temper_hbm, row_vec_hbm, col_vec_hbm,
    out,
    col_in, row_len, col_len, valid, temper, row_vec, col_vec,
    row_buf, col_buf, col_nat,
    ql, kt, qt, vt, qf, kf, rv, cv,
    scores, e_row, e_col, row_acc, col_acc,
    row_res, row_got, col_msg, col_got, order, eye, pick,
    in_sem, far_send, far_recv, near_send, near_recv, row_send, row_recv, twin_send, twin_recv, own_sem,
    rres_send, rres_recv, cres_send, cres_recv,
):
    r = lax.axis_index("row")
    c = lax.axis_index("col")
    z, x, yh = r // 8, lax.rem(r // 2, 4), lax.rem(r, 2)
    yl, core = c // 2, lax.rem(c, 2)
    zh = z // 4

    def device(dz, dx, dyh):
        return (lax.rem(z + dz, 8) * 8 + lax.rem(x + dx, 4) * 2 + lax.rem(yh + dyh, 2), c)

    def near(k, back):
        kz = k // 4
        dz = jnp.where(kz == 3, jnp.where((core == 0) != back, 2, 6), jnp.where(kz == 2, 7, kz))
        dx = lax.rem(k, 4)
        return device(dz, 4 - dx if back else dx, 0)

    other_y, other_z = device(0, 0, 1), device(4, 0, 0)

    def along(k):
        return (r, lax.rem(yl + k, 4) * 2 + core)

    twin = (r, yl * 2 + 1 - core)

    barrier = pltpu.get_barrier_semaphore()

    def greet(target):
        pl.semaphore_signal(barrier, inc=1, device_id=target, device_id_type=MESH)
        return 0

    greet(other_y)
    greet(other_z)
    lax.fori_loop(1, 16, lambda k, _: greet(near(k, True)), 0)
    lax.fori_loop(1, 4, lambda k, _: greet(along(k)), 0)
    greet(twin)

    small = [(col_hbm, col_in), (row_len_hbm, row_len), (col_len_hbm, col_len), (valid_hbm, valid),
             (temper_hbm, temper), (row_vec_hbm, row_vec), (col_vec_hbm, col_vec)]
    copies = [pltpu.make_async_copy(src, dst, in_sem.at[n]) for n, (src, dst) in enumerate(small)]
    for copy in copies:
        copy.start()
    own_rows = pl.ds(pl.multiple_of(core * 128 + yl * 32, 32), 32)
    own_row_copy = pltpu.make_async_copy(row_hbm, row_buf.at[:, own_rows, :], own_sem)
    own_row_copy.start()

    for copy in copies:
        copy.wait()
    block = (lax.rem(z, 4) * 4 + x) * 4
    slot = block + zh * 2 + yh
    col_buf[slot] = jnp.concatenate([col_in[j].astype(f32) for j in range(C)], axis=0).astype(bf16)

    pl.semaphore_wait(barrier, 21)

    def send_far(span, n, target):
        pltpu.make_async_remote_copy(
            src_ref=col_buf.at[span], dst_ref=col_buf.at[span],
            send_sem=far_send.at[n], recv_sem=far_recv.at[n],
            device_id=target, device_id_type=MESH).start()

    send_far(pl.ds(slot, 1), 0, other_y)

    def send_rows(t):
        half = pl.ds(t * 128, 128)

        def one(k, _):
            pltpu.make_async_remote_copy(
                src_ref=row_hbm.at[:, :, half], dst_ref=row_buf.at[:, own_rows, half],
                send_sem=row_send, recv_sem=row_recv.at[t],
                device_id=along(k), device_id_type=MESH).start()
            return 0

        lax.fori_loop(1, 4, one, 0)

    def send_near(part):
        pair = pl.ds(block + part * 2, 2)

        def one(k, _):
            pltpu.make_async_remote_copy(
                src_ref=col_buf.at[pair], dst_ref=col_buf.at[pair],
                send_sem=near_send, recv_sem=near_recv,
                device_id=near(k, False), device_id_type=MESH).start()
            return 0

        lax.fori_loop(1, 16, one, 0)

    def await_far(n):
        theirs = col_buf.at[pl.ds(0, n + 1)]
        pltpu.make_async_copy(theirs, theirs, far_recv.at[n]).wait()

    same_core = pl.ds(pl.multiple_of(core * 128, 128), 128)

    def pass_rows(t):
        half = pl.ds(t * 128, 128)
        three = row_buf.at[:, pl.ds(0, 96), half]
        pltpu.make_async_copy(three, three, row_recv.at[t]).wait()
        pltpu.make_async_remote_copy(
            src_ref=row_buf.at[:, same_core, half], dst_ref=row_buf.at[:, same_core, half],
            send_sem=twin_send, recv_sem=twin_recv.at[t],
            device_id=twin, device_id_type=MESH).start()

    send_rows(0)
    send_rows(1)
    await_far(0)
    send_far(pl.ds(block + zh * 2, 2), 1, other_z)
    send_near(zh)
    own_row_copy.wait()
    pass_rows(0)
    await_far(1)
    send_near(1 - zh)
    pass_rows(1)

    rv[...] = jnp.broadcast_to(row_vec[...], (L, H)).T.reshape(NH, D, L)
    cv[...] = jnp.broadcast_to(col_vec[...], (L, H)).T.reshape(NH, D, L)
    row_acc[...] = jnp.zeros_like(row_acc)
    col_acc[...] = jnp.zeros_like(col_acc)

    def row_residue(place):
        return (lax.rem(place // 32, 4) * 2 + place // 128) * 32 + lax.rem(place, 32)

    def col_residue(place):
        s = place // 4
        device_z = s // 16 + lax.rem(s // 2, 2) * 4
        return ((device_z * 4 + lax.rem(s // 4, 4)) * 2 + lax.rem(s, 2)) * 4 + lax.rem(place, 4)

    lane = lax.broadcasted_iota(jnp.int32, (1, L), 1)
    row_lane, col_lane = row_residue(lane), col_residue(lane)
    row_sub = row_residue(lax.broadcasted_iota(jnp.int32, (L, 1), 0))
    lane128 = lax.broadcasted_iota(jnp.int32, (1, 128), 1)

    def prepare_rows(t):
        half = pl.ds(t * 128, 128)
        theirs = row_buf.at[:, pl.ds(0, 128), half]
        pltpu.make_async_copy(theirs, theirs, twin_recv.at[t]).wait()
        scale = jnp.zeros((1, 128), f32)
        for g in range(HT):
            scale = jnp.where(lane128 // D == g, temper[t * HT + g] * LOG2E, scale)

        def one(i, _):
            q = row_buf[i, :, half].astype(f32)
            ok = row_sub < row_len[i]
            filled = jnp.where(ok, q, q[0:1]) * scale
            hi = filled.astype(bf16).astype(f32)
            lo = filled - hi
            for g in range(HT):
                mine = lane128 // D == g
                ql[i, t * HT + g, :, 0:128] = jnp.where(mine, hi, 0.0).astype(bf16)
                ql[i, t * HT + g, :, 128:256] = jnp.where(mine, lo, 0.0).astype(bf16)
            flat = jnp.where(ok, q, 0.0).T
            ones = jnp.where(row_lane < row_len[i], 1.0, 0.0)
            pad = jnp.zeros((15, L), f32)
            for g in range(HT):
                own = flat[g * D:(g + 1) * D]
                qf[i, t * HT + g] = own
                qt[i, t * HT + g] = jnp.concatenate([own, ones, pad], axis=0).astype(bf16)
            return 0

        lax.fori_loop(0, R, one, 0)

    def prepare_cols(t):
        for g in range(4):
            piece = col_buf[g * 16:(g + 1) * 16, :, t * 128:(t + 1) * 128].reshape(256, 128)
            moved = dot(order[...], piece).astype(bf16)
            for j in range(C):
                col_nat[j, g * 64:(g + 1) * 64, :] = moved[j * 64:(j + 1) * 64]
        pad = jnp.zeros((15, L), f32)
        for j in range(C):
            flat = dot_t(eye[...], col_nat[j])
            ok = col_lane < col_len[j]
            filled = jnp.where(ok, flat, flat[:, 0:1]).astype(bf16)
            span = pl.ds((j % 2) * L, L)
            kt[j // 2, t, 0:128, span] = filled
            kt[j // 2, t, 128:256, span] = filled
            flat = jnp.where(ok, flat, 0.0)
            ones = jnp.where(ok, 1.0, 0.0)
            for g in range(HT):
                own = flat[g * D:(g + 1) * D]
                kf[j // 2, t * HT + g, :, span] = own
                vt[j, t * HT + g] = jnp.concatenate([own, ones, pad], axis=0).astype(bf16)

    def place(s):
        s = jnp.maximum(s, 0)
        return s // (2 * R), lax.rem(s // R, 2), lax.rem(s, R)

    def stage_scores(s, g):
        t, jp, i = place(s)
        scores[g] = dot(ql[i, t * HT + g], kt[jp, t])

    def stage_weights(g):
        for u in range(2):
            block = scores[g, :, u * L:(u + 1) * L]
            e_row[g, u] = jnp.exp2(block - jnp.max(block, axis=1, keepdims=True)).astype(bf16)
            e_col[g, :, u * L:(u + 1) * L] = jnp.exp2(block - jnp.max(block, axis=0, keepdims=True)).astype(bf16)

    def readout(product, own, vector):
        term = jnp.tanh(product[:D] * (1.0 / product[D:D + 1]) + own) * vector
        return term[0:8] + term[8:16] + term[16:24] + term[24:32]

    def stage_sums(s, g):
        t, jp, i = place(s)
        h = t * HT + g
        toward_rows = dot(qt[i, h], e_col[g])
        sides = [dot_t(vt[jp * 2 + u, h], e_row[g, u]) for u in range(2)]
        real = s >= 0
        for u in range(2):
            weight = valid[i, jp * 2 + u].astype(f32)
            span = pl.ds(u * L, L)
            row_term = readout(sides[u], qf[i, h], rv[h]) * weight
            col_term = readout(toward_rows[:, u * L:(u + 1) * L], kf[jp, h, :, span], cv[h]) * weight
            row_acc[i] += jnp.where(real, row_term, 0.0)
            col_acc[jp, :, span] += jnp.where(real, col_term, 0.0)

    prepare_rows(0)
    prepare_rows(1)
    o = lax.broadcasted_iota(jnp.int32, (256, 256), 0)
    m = lax.broadcasted_iota(jnp.int32, (256, 256), 1)
    source = lax.rem(o // 4, 16) * 16 + (o // 64) * 4 + lax.rem(o, 4)
    order[...] = jnp.where(m == source, 1.0, 0.0).astype(bf16)
    eye[...] = jnp.where(lax.broadcasted_iota(jnp.int32, (128, 128), 0)
                         == lax.broadcasted_iota(jnp.int32, (128, 128), 1), 1.0, 0.0).astype(bf16)
    from_b = lax.broadcasted_iota(jnp.int32, (3 * L, 128), 0)
    to_lane = lax.broadcasted_iota(jnp.int32, (3 * L, 128), 1)
    pick[...] = jnp.where(to_lane == lax.rem(from_b, 4), 1.0, 0.0).astype(bf16)
    theirs = col_buf.at[pl.ds(0, 60)]
    pltpu.make_async_copy(theirs, theirs, near_recv).wait()
    prepare_cols(0)

    def steps(n, _):
        @pl.when(n == STEPS // UNROLL // 2)
        def _():
            prepare_cols(1)

        for i in range(UNROLL):
            s = n * UNROLL + i
            for g in range(HT):
                stage_scores(s, g)
                stage_weights((g + 3) % 4)
                stage_sums(s if g >= 2 else s - 1, (g + 2) % 4)
        return 0

    lax.fori_loop(0, STEPS // UNROLL, steps, 0)
    stage_weights(3)
    stage_sums(STEPS - 1, 2)
    stage_sums(STEPS - 1, 3)

    row_scale = 1.0 / math.sqrt(C * N_COL)
    col_scale = 1.0 / math.sqrt(R * N_ROW)
    for i in range(R):
        total = jnp.sum(row_acc[i], axis=0, keepdims=True) * row_scale
        total = jnp.where(row_lane < row_len[i], total, 0.0)
        for t in range(2):
            row_res[t, i:i + 1, :] = total[:, t * 128:(t + 1) * 128]
    row_res[:, R:8, :] = jnp.zeros((2, 8 - R, 128), f32)

    dest = lax.broadcasted_iota(jnp.int32, (N_ROW, L), 0)
    mine = lax.broadcasted_iota(jnp.int32, (N_ROW, L), 1) // 4 == dest
    spread = []
    for j in range(C):
        total = jnp.sum(col_acc[j // 2, :, (j % 2) * L:(j % 2 + 1) * L], axis=0, keepdims=True) * col_scale
        total = jnp.where(col_lane < col_len[j], total, 0.0)
        parts = []
        for _ in range(3):
            parts.append(total.astype(bf16).astype(f32))
            total = total - parts[-1]
        spread.append(jnp.concatenate([jnp.where(mine, part, 0.0).astype(bf16) for part in parts], axis=1))
    picked = dot(jnp.concatenate(spread, axis=0), pick[...])
    msg = picked[0:N_ROW]
    for j in range(1, C):
        msg = msg + pltpu.roll(picked[j * N_ROW:(j + 1) * N_ROW], 4 * j, 1)
    col_msg[...] = msg.reshape(N_ROW, 1, 128)

    def send_col_res(k, _):
        n, m = k // 8, lax.rem(k, 8)
        dz = lax.rem(12 + jnp.where(lax.rem(n, 2) == 1, -((n + 1) // 2), n // 2), 8)
        dx, dyh = lax.rem(m // 2 + 2, 4), lax.rem(m + 1, 2)
        to_z, to_x, to_yh = lax.rem(z + dz, 8), lax.rem(x + dx, 4), lax.rem(yh + dyh, 2)
        place = (lax.rem(to_z, 4) * 4 + to_x) * 4 + (to_z // 4) * 2 + to_yh
        pltpu.make_async_remote_copy(
            src_ref=col_msg.at[place], dst_ref=col_got.at[r],
            send_sem=cres_send, recv_sem=cres_recv,
            device_id=device(dz, dx, dyh), device_id_type=MESH).start()
        return 0

    def send_row_res(k, _):
        to = lax.rem(c + k, N_COL)
        pltpu.make_async_remote_copy(
            src_ref=row_res.at[lax.rem(to, 2)], dst_ref=row_got.at[c],
            send_sem=rres_send, recv_sem=rres_recv,
            device_id=(r, to), device_id_type=MESH).start()
        return 0

    lax.fori_loop(0, 61, send_col_res, 0)
    lax.fori_loop(62, 64, send_col_res, 0)
    lax.fori_loop(1, N_COL, send_row_res, 0)
    pltpu.make_async_copy(col_msg.at[slot], col_got.at[r], cres_recv).start()
    pltpu.make_async_copy(row_res.at[core], row_got.at[c], rres_recv).start()

    pltpu.make_async_copy(row_got, row_got, rres_recv).wait()
    total = row_got[0]
    for k in range(1, N_COL):
        total = total + row_got[k]
    quarter = yl
    answer = total[0:R, 0:32]
    for g in range(1, 4):
        answer = jnp.where(quarter == g, total[0:R, g * 32:(g + 1) * 32], answer)
    out[0:R, 0:32] = answer

    pltpu.make_async_copy(col_got, col_got, cres_recv).wait()
    total = jnp.sum(col_got[...], axis=0)
    for j in range(C):
        out[R + j:R + j + 1, 0:4] = total[:, j * 4:(j + 1) * 4]

    for n in range(2):
        sent = col_buf.at[pl.ds(0, n + 1)]
        pltpu.make_async_copy(sent, sent, far_send.at[n]).wait()
    sent = col_buf.at[pl.ds(0, 60)]
    pltpu.make_async_copy(sent, sent, near_send).wait()
    most = row_buf.at[:, pl.ds(0, 96), :]
    pltpu.make_async_copy(most, most, row_send).wait()
    most = row_buf.at[:, pl.ds(0, 128), :]
    pltpu.make_async_copy(most, most, twin_send).wait()
    others = pl.ds(0, N_ROW - 1)
    pltpu.make_async_copy(col_got.at[others], col_got.at[others], cres_send).wait()
    others = pl.ds(0, N_COL - 1)
    pltpu.make_async_copy(row_got.at[others], row_got.at[others], rres_send).wait()


def part_results(result, row_out, col_out):
    row_out[...] = result[0:R, 0:32]
    col_out[...] = result[R:R + C, 0:4]


def body(row_embed, col_embed, row_length, col_length, pair_valid, temper, row_vector, col_vector):
    vmem = pl.BlockSpec(memory_space=pltpu.VMEM)
    hbm = pl.BlockSpec(memory_space=pltpu.HBM)
    dma = pltpu.SemaphoreType.DMA
    result = pl.pallas_call(
        kernel,
        out_shape=jax.ShapeDtypeStruct((R + C, 128), f32),
        in_specs=[hbm] * 8,
        out_specs=vmem,
        scratch_shapes=[
            pltpu.VMEM((C, 4, H), bf16),
            pltpu.SMEM((R,), jnp.int32),
            pltpu.SMEM((C,), jnp.int32),
            pltpu.SMEM((R, C), jnp.int32),
            pltpu.SMEM((NH,), f32),
            pltpu.VMEM((1, H), f32),
            pltpu.VMEM((1, H), f32),
            pltpu.VMEM((R, L, H), bf16),
            pltpu.VMEM((N_ROW, 16, H), bf16),
            pltpu.VMEM((C, L, 128), bf16),
            pltpu.VMEM((R, NH, L, 256), bf16),
            pltpu.VMEM((C // 2, 2, 256, 2 * L), bf16),
            pltpu.VMEM((R, NH, 48, L), bf16),
            pltpu.VMEM((C, NH, 48, L), bf16),
            pltpu.VMEM((R, NH, D, L), f32),
            pltpu.VMEM((C // 2, NH, D, 2 * L), f32),
            pltpu.VMEM((NH, D, L), f32),
            pltpu.VMEM((NH, D, L), f32),
            pltpu.VMEM((HT, L, 2 * L), f32),
            pltpu.VMEM((HT, 2, L, L), bf16),
            pltpu.VMEM((HT, L, 2 * L), bf16),
            pltpu.VMEM((R, 8, L), f32),
            pltpu.VMEM((C // 2, 8, 2 * L), f32),
            pltpu.VMEM((2, 8, 128), f32),
            pltpu.VMEM((N_COL, 8, 128), f32),
            pltpu.VMEM((N_ROW, 1, 128), f32),
            pltpu.VMEM((N_ROW, 1, 128), f32),
            pltpu.VMEM((256, 256), bf16),
            pltpu.VMEM((128, 128), bf16),
            pltpu.VMEM((3 * L, 128), bf16),
            dma((7,)), dma((2,)), dma((2,)), dma, dma, dma, dma((2,)), dma, dma((2,)), dma,
            dma, dma, dma, dma,
        ],
        compiler_params=pltpu.CompilerParams(
            collective_id=0, has_side_effects=True, vmem_limit_bytes=64 * 2**20),
    )(row_embed, col_embed, row_length, col_length, pair_valid, temper,
      row_vector.reshape(1, H), col_vector.reshape(1, H))
    return pl.pallas_call(
        part_results,
        out_shape=[jax.ShapeDtypeStruct((R, 32), f32), jax.ShapeDtypeStruct((C, 4), f32)],
        in_specs=[vmem],
        out_specs=[vmem, vmem],
    )(result)


def solution(mesh):
    in_specs = (
        P("row", "col", None),
        P("col", "row", None),
        P("row"),
        P("col"),
        P("row", "col"),
        P(),
        P(),
        P(),
    )
    out_specs = (P("row", "col"), P("col", "row"))
    return jax.shard_map(body, mesh=mesh, in_specs=in_specs, out_specs=out_specs, check_vma=False)
```

```python
import functools
import math

import jax
import jax.numpy as jnp
from jax import lax
from jax.experimental import pallas as pl
from jax.experimental.pallas import tpu as pltpu
from jax.sharding import PartitionSpec as P

MESH = pl.DeviceIdType.MESH
f32 = jnp.float32
bf16 = jnp.bfloat16
LOG2E = math.log2(math.e)

N_ROW = 64
N_COL = 8
R = 4
C = 4
L = 256
H = 256
NH = 8
D = H // NH
HT = 128 // D
STEPS = 2 * (C // 2) * R
UNROLL = 4


def dot(a, b):
    return jnp.dot(a, b, preferred_element_type=f32)


def dot_t(a, b):
    return lax.dot_general(a, b, (((1,), (1,)), ((), ())), preferred_element_type=f32)


def kernel(
    row_hbm, col_hbm, row_len_hbm, col_len_hbm, valid_hbm, temper_hbm, row_vec_hbm, col_vec_hbm,
    out,
    col_in, row_len, col_len, valid, temper, row_vec, col_vec,
    row_buf, col_buf, col_nat,
    ql, kt, qt, vt, qf, kf, rv, cv,
    scores, e_row, e_col, row_acc, col_acc,
    row_res, row_got, col_msg, col_got, order, eye, pick,
    in_sem, far_send, far_recv, near_send, near_recv, row_send, row_recv, twin_send, twin_recv, own_sem,
    rres_send, rres_recv, cres_send, cres_recv,
):
    r = lax.axis_index("row")
    c = lax.axis_index("col")
    z, x, yh = r // 8, lax.rem(r // 2, 4), lax.rem(r, 2)
    yl, core = c // 2, lax.rem(c, 2)
    zh = z // 4

    def device(dz, dx, dyh):
        return (lax.rem(z + dz, 8) * 8 + lax.rem(x + dx, 4) * 2 + lax.rem(yh + dyh, 2), c)

    def near(k, back):
        kz = k // 4
        dz = jnp.where(kz == 3, jnp.where((core == 0) != back, 2, 6), jnp.where(kz == 2, 7, kz))
        dx = lax.rem(k, 4)
        return device(dz, 4 - dx if back else dx, 0)

    other_y, other_z = device(0, 0, 1), device(4, 0, 0)

    def along(k):
        return (r, lax.rem(yl + k, 4) * 2 + core)

    twin = (r, yl * 2 + 1 - core)

    barrier = pltpu.get_barrier_semaphore()

    def greet(target):
        pl.semaphore_signal(barrier, inc=1, device_id=target, device_id_type=MESH)
        return 0

    greet(other_y)
    greet(other_z)
    lax.fori_loop(1, 16, lambda k, _: greet(near(k, True)), 0)
    lax.fori_loop(1, 4, lambda k, _: greet(along(k)), 0)
    greet(twin)

    small = [(col_hbm, col_in), (row_len_hbm, row_len), (col_len_hbm, col_len), (valid_hbm, valid),
             (temper_hbm, temper), (row_vec_hbm, row_vec), (col_vec_hbm, col_vec)]
    copies = [pltpu.make_async_copy(src, dst, in_sem.at[n]) for n, (src, dst) in enumerate(small)]
    for copy in copies:
        copy.start()
    own_rows = pl.ds(pl.multiple_of(core * 128 + yl * 32, 32), 32)
    own_row_copy = pltpu.make_async_copy(row_hbm, row_buf.at[:, own_rows, :], own_sem)
    own_row_copy.start()

    for copy in copies:
        copy.wait()
    block = (lax.rem(z, 4) * 4 + x) * 4
    slot = block + zh * 2 + yh
    col_buf[slot] = jnp.concatenate([col_in[j].astype(f32) for j in range(C)], axis=0).astype(bf16)

    pl.semaphore_wait(barrier, 21)

    def send_far(span, n, target):
        pltpu.make_async_remote_copy(
            src_ref=col_buf.at[span], dst_ref=col_buf.at[span],
            send_sem=far_send.at[n], recv_sem=far_recv.at[n],
            device_id=target, device_id_type=MESH).start()

    send_far(pl.ds(slot, 1), 0, other_y)

    def send_rows(t):
        half = pl.ds(t * 128, 128)

        def one(k, _):
            pltpu.make_async_remote_copy(
                src_ref=row_hbm.at[:, :, half], dst_ref=row_buf.at[:, own_rows, half],
                send_sem=row_send, recv_sem=row_recv.at[t],
                device_id=along(k), device_id_type=MESH).start()
            return 0

        lax.fori_loop(1, 4, one, 0)

    def send_near(part):
        pair = pl.ds(block + part * 2, 2)

        def one(k, _):
            pltpu.make_async_remote_copy(
                src_ref=col_buf.at[pair], dst_ref=col_buf.at[pair],
                send_sem=near_send, recv_sem=near_recv,
                device_id=near(k, False), device_id_type=MESH).start()
            return 0

        lax.fori_loop(1, 16, one, 0)

    def await_far(n):
        theirs = col_buf.at[pl.ds(0, n + 1)]
        pltpu.make_async_copy(theirs, theirs, far_recv.at[n]).wait()

    same_core = pl.ds(pl.multiple_of(core * 128, 128), 128)

    def pass_rows(t):
        half = pl.ds(t * 128, 128)
        three = row_buf.at[:, pl.ds(0, 96), half]
        pltpu.make_async_copy(three, three, row_recv.at[t]).wait()
        pltpu.make_async_remote_copy(
            src_ref=row_buf.at[:, same_core, half], dst_ref=row_buf.at[:, same_core, half],
            send_sem=twin_send, recv_sem=twin_recv.at[t],
            device_id=twin, device_id_type=MESH).start()

    send_rows(0)
    send_rows(1)
    await_far(0)
    send_far(pl.ds(block + zh * 2, 2), 1, other_z)
    send_near(zh)
    await_far(1)
    send_near(1 - zh)
    own_row_copy.wait()
    pass_rows(0)
    pass_rows(1)

    rv[...] = jnp.broadcast_to(row_vec[...], (L, H)).T.reshape(NH, D, L)
    cv[...] = jnp.broadcast_to(col_vec[...], (L, H)).T.reshape(NH, D, L)
    row_acc[...] = jnp.zeros_like(row_acc)
    col_acc[...] = jnp.zeros_like(col_acc)

    def row_residue(place):
        return (lax.rem(place // 32, 4) * 2 + place // 128) * 32 + lax.rem(place, 32)

    def col_residue(place):
        s = place // 4
        device_z = s // 16 + lax.rem(s // 2, 2) * 4
        return ((device_z * 4 + lax.rem(s // 4, 4)) * 2 + lax.rem(s, 2)) * 4 + lax.rem(place, 4)

    lane = lax.broadcasted_iota(jnp.int32, (1, L), 1)
    row_lane, col_lane = row_residue(lane), col_residue(lane)
    row_sub = row_residue(lax.broadcasted_iota(jnp.int32, (L, 1), 0))
    lane128 = lax.broadcasted_iota(jnp.int32, (1, 128), 1)

    def prepare_rows(t):
        half = pl.ds(t * 128, 128)
        theirs = row_buf.at[:, pl.ds(0, 128), half]
        pltpu.make_async_copy(theirs, theirs, twin_recv.at[t]).wait()
        scale = jnp.zeros((1, 128), f32)
        for g in range(HT):
            scale = jnp.where(lane128 // D == g, temper[t * HT + g] * LOG2E, scale)

        def one(i, _):
            q = row_buf[i, :, half].astype(f32)
            ok = row_sub < row_len[i]
            filled = jnp.where(ok, q, q[0:1]) * scale
            hi = filled.astype(bf16).astype(f32)
            lo = filled - hi
            for g in range(HT):
                mine = lane128 // D == g
                ql[i, t * HT + g, :, 0:128] = jnp.where(mine, hi, 0.0).astype(bf16)
                ql[i, t * HT + g, :, 128:256] = jnp.where(mine, lo, 0.0).astype(bf16)
            flat = jnp.where(ok, q, 0.0).T
            ones = jnp.where(row_lane < row_len[i], 1.0, 0.0)
            pad = jnp.zeros((15, L), f32)
            for g in range(HT):
                own = flat[g * D:(g + 1) * D]
                qf[i, t * HT + g] = own
                qt[i, t * HT + g] = jnp.concatenate([own, ones, pad], axis=0).astype(bf16)
            return 0

        lax.fori_loop(0, R, one, 0)

    def prepare_cols(t):
        for g in range(4):
            piece = col_buf[g * 16:(g + 1) * 16, :, t * 128:(t + 1) * 128].reshape(256, 128)
            moved = dot(order[...], piece).astype(bf16)
            for j in range(C):
                col_nat[j, g * 64:(g + 1) * 64, :] = moved[j * 64:(j + 1) * 64]
        pad = jnp.zeros((15, L), f32)
        for j in range(C):
            flat = dot_t(eye[...], col_nat[j])
            ok = col_lane < col_len[j]
            filled = jnp.where(ok, flat, flat[:, 0:1]).astype(bf16)
            span = pl.ds((j % 2) * L, L)
            kt[j // 2, t, 0:128, span] = filled
            kt[j // 2, t, 128:256, span] = filled
            flat = jnp.where(ok, flat, 0.0)
            ones = jnp.where(ok, 1.0, 0.0)
            for g in range(HT):
                own = flat[g * D:(g + 1) * D]
                kf[j // 2, t * HT + g, :, span] = own
                vt[j, t * HT + g] = jnp.concatenate([own, ones, pad], axis=0).astype(bf16)

    def place(s):
        s = jnp.maximum(s, 0)
        return s // (2 * R), lax.rem(s // R, 2), lax.rem(s, R)

    def stage_scores(s, g):
        t, jp, i = place(s)
        scores[g] = dot(ql[i, t * HT + g], kt[jp, t])

    def stage_weights(g):
        for u in range(2):
            block = scores[g, :, u * L:(u + 1) * L]
            e_row[g, u] = jnp.exp2(block - jnp.max(block, axis=1, keepdims=True)).astype(bf16)
            e_col[g, :, u * L:(u + 1) * L] = jnp.exp2(block - jnp.max(block, axis=0, keepdims=True)).astype(bf16)

    def readout(product, own, vector):
        term = jnp.tanh(product[:D] * (1.0 / product[D:D + 1]) + own) * vector
        return term[0:8] + term[8:16] + term[16:24] + term[24:32]

    def stage_sums(s, g):
        t, jp, i = place(s)
        h = t * HT + g
        toward_rows = dot(qt[i, h], e_col[g])
        sides = [dot_t(vt[jp * 2 + u, h], e_row[g, u]) for u in range(2)]
        real = s >= 0
        for u in range(2):
            weight = valid[i, jp * 2 + u].astype(f32)
            span = pl.ds(u * L, L)
            row_term = readout(sides[u], qf[i, h], rv[h]) * weight
            col_term = readout(toward_rows[:, u * L:(u + 1) * L], kf[jp, h, :, span], cv[h]) * weight
            row_acc[i] += jnp.where(real, row_term, 0.0)
            col_acc[jp, :, span] += jnp.where(real, col_term, 0.0)

    prepare_rows(0)
    prepare_rows(1)
    o = lax.broadcasted_iota(jnp.int32, (256, 256), 0)
    m = lax.broadcasted_iota(jnp.int32, (256, 256), 1)
    source = lax.rem(o // 4, 16) * 16 + (o // 64) * 4 + lax.rem(o, 4)
    order[...] = jnp.where(m == source, 1.0, 0.0).astype(bf16)
    eye[...] = jnp.where(lax.broadcasted_iota(jnp.int32, (128, 128), 0)
                         == lax.broadcasted_iota(jnp.int32, (128, 128), 1), 1.0, 0.0).astype(bf16)
    from_b = lax.broadcasted_iota(jnp.int32, (3 * L, 128), 0)
    to_lane = lax.broadcasted_iota(jnp.int32, (3 * L, 128), 1)
    pick[...] = jnp.where(to_lane == lax.rem(from_b, 4), 1.0, 0.0).astype(bf16)
    theirs = col_buf.at[pl.ds(0, 60)]
    pltpu.make_async_copy(theirs, theirs, near_recv).wait()
    prepare_cols(0)

    def steps(n, _):
        @pl.when(n == STEPS // UNROLL // 2)
        def _():
            prepare_cols(1)

        for i in range(UNROLL):
            s = n * UNROLL + i
            for g in range(HT):
                stage_scores(s, g)
                stage_weights((g + 3) % 4)
                stage_sums(s if g >= 2 else s - 1, (g + 2) % 4)
        return 0

    lax.fori_loop(0, STEPS // UNROLL, steps, 0)
    stage_weights(3)
    stage_sums(STEPS - 1, 2)
    stage_sums(STEPS - 1, 3)

    row_scale = 1.0 / math.sqrt(C * N_COL)
    col_scale = 1.0 / math.sqrt(R * N_ROW)
    for i in range(R):
        total = jnp.sum(row_acc[i], axis=0, keepdims=True) * row_scale
        total = jnp.where(row_lane < row_len[i], total, 0.0)
        for t in range(2):
            row_res[t, i:i + 1, :] = total[:, t * 128:(t + 1) * 128]
    row_res[:, R:8, :] = jnp.zeros((2, 8 - R, 128), f32)

    dest = lax.broadcasted_iota(jnp.int32, (N_ROW, L), 0)
    mine = lax.broadcasted_iota(jnp.int32, (N_ROW, L), 1) // 4 == dest
    spread = []
    for j in range(C):
        total = jnp.sum(col_acc[j // 2, :, (j % 2) * L:(j % 2 + 1) * L], axis=0, keepdims=True) * col_scale
        total = jnp.where(col_lane < col_len[j], total, 0.0)
        parts = []
        for _ in range(3):
            parts.append(total.astype(bf16).astype(f32))
            total = total - parts[-1]
        spread.append(jnp.concatenate([jnp.where(mine, part, 0.0).astype(bf16) for part in parts], axis=1))
    picked = dot(jnp.concatenate(spread, axis=0), pick[...])
    msg = picked[0:N_ROW]
    for j in range(1, C):
        msg = msg + pltpu.roll(picked[j * N_ROW:(j + 1) * N_ROW], 4 * j, 1)
    col_msg[...] = msg.reshape(N_ROW, 1, 128)

    def send_col_res(k, _):
        n, m = k // 8, lax.rem(k, 8)
        dz = lax.rem(12 + jnp.where(lax.rem(n, 2) == 1, -((n + 1) // 2), n // 2), 8)
        dx, dyh = lax.rem(m // 2 + 2, 4), lax.rem(m + 1, 2)
        to_z, to_x, to_yh = lax.rem(z + dz, 8), lax.rem(x + dx, 4), lax.rem(yh + dyh, 2)
        place = (lax.rem(to_z, 4) * 4 + to_x) * 4 + (to_z // 4) * 2 + to_yh
        pltpu.make_async_remote_copy(
            src_ref=col_msg.at[place], dst_ref=col_got.at[r],
            send_sem=cres_send, recv_sem=cres_recv,
            device_id=device(dz, dx, dyh), device_id_type=MESH).start()
        return 0

    def send_row_res(k, _):
        to = lax.rem(c + k, N_COL)
        pltpu.make_async_remote_copy(
            src_ref=row_res.at[lax.rem(to, 2)], dst_ref=row_got.at[c],
            send_sem=rres_send, recv_sem=rres_recv,
            device_id=(r, to), device_id_type=MESH).start()
        return 0

    lax.fori_loop(0, 61, send_col_res, 0)
    lax.fori_loop(62, 64, send_col_res, 0)
    lax.fori_loop(1, N_COL, send_row_res, 0)
    pltpu.make_async_copy(col_msg.at[slot], col_got.at[r], cres_recv).start()
    pltpu.make_async_copy(row_res.at[core], row_got.at[c], rres_recv).start()

    pltpu.make_async_copy(row_got, row_got, rres_recv).wait()
    total = row_got[0]
    for k in range(1, N_COL):
        total = total + row_got[k]
    quarter = yl
    answer = total[0:R, 0:32]
    for g in range(1, 4):
        answer = jnp.where(quarter == g, total[0:R, g * 32:(g + 1) * 32], answer)
    out[0:R, 0:32] = answer

    pltpu.make_async_copy(col_got, col_got, cres_recv).wait()
    total = jnp.sum(col_got[...], axis=0)
    for j in range(C):
        out[R + j:R + j + 1, 0:4] = total[:, j * 4:(j + 1) * 4]

    for n in range(2):
        sent = col_buf.at[pl.ds(0, n + 1)]
        pltpu.make_async_copy(sent, sent, far_send.at[n]).wait()
    sent = col_buf.at[pl.ds(0, 60)]
    pltpu.make_async_copy(sent, sent, near_send).wait()
    most = row_buf.at[:, pl.ds(0, 96), :]
    pltpu.make_async_copy(most, most, row_send).wait()
    most = row_buf.at[:, pl.ds(0, 128), :]
    pltpu.make_async_copy(most, most, twin_send).wait()
    others = pl.ds(0, N_ROW - 1)
    pltpu.make_async_copy(col_got.at[others], col_got.at[others], cres_send).wait()
    others = pl.ds(0, N_COL - 1)
    pltpu.make_async_copy(row_got.at[others], row_got.at[others], rres_send).wait()


def part_results(result, row_out, col_out):
    row_out[...] = result[0:R, 0:32]
    col_out[...] = result[R:R + C, 0:4]


def body(row_embed, col_embed, row_length, col_length, pair_valid, temper, row_vector, col_vector):
    vmem = pl.BlockSpec(memory_space=pltpu.VMEM)
    hbm = pl.BlockSpec(memory_space=pltpu.HBM)
    dma = pltpu.SemaphoreType.DMA
    result = pl.pallas_call(
        kernel,
        out_shape=jax.ShapeDtypeStruct((R + C, 128), f32),
        in_specs=[hbm] * 8,
        out_specs=vmem,
        scratch_shapes=[
            pltpu.VMEM((C, 4, H), bf16),
            pltpu.SMEM((R,), jnp.int32),
            pltpu.SMEM((C,), jnp.int32),
            pltpu.SMEM((R, C), jnp.int32),
            pltpu.SMEM((NH,), f32),
            pltpu.VMEM((1, H), f32),
            pltpu.VMEM((1, H), f32),
            pltpu.VMEM((R, L, H), bf16),
            pltpu.VMEM((N_ROW, 16, H), bf16),
            pltpu.VMEM((C, L, 128), bf16),
            pltpu.VMEM((R, NH, L, 256), bf16),
            pltpu.VMEM((C // 2, 2, 256, 2 * L), bf16),
            pltpu.VMEM((R, NH, 48, L), bf16),
            pltpu.VMEM((C, NH, 48, L), bf16),
            pltpu.VMEM((R, NH, D, L), f32),
            pltpu.VMEM((C // 2, NH, D, 2 * L), f32),
            pltpu.VMEM((NH, D, L), f32),
            pltpu.VMEM((NH, D, L), f32),
            pltpu.VMEM((HT, L, 2 * L), f32),
            pltpu.VMEM((HT, 2, L, L), bf16),
            pltpu.VMEM((HT, L, 2 * L), bf16),
            pltpu.VMEM((R, 8, L), f32),
            pltpu.VMEM((C // 2, 8, 2 * L), f32),
            pltpu.VMEM((2, 8, 128), f32),
            pltpu.VMEM((N_COL, 8, 128), f32),
            pltpu.VMEM((N_ROW, 1, 128), f32),
            pltpu.VMEM((N_ROW, 1, 128), f32),
            pltpu.VMEM((256, 256), bf16),
            pltpu.VMEM((128, 128), bf16),
            pltpu.VMEM((3 * L, 128), bf16),
            dma((7,)), dma((2,)), dma((2,)), dma, dma, dma, dma((2,)), dma, dma((2,)), dma,
            dma, dma, dma, dma,
        ],
        compiler_params=pltpu.CompilerParams(
            collective_id=0, has_side_effects=True, vmem_limit_bytes=64 * 2**20),
    )(row_embed, col_embed, row_length, col_length, pair_valid, temper,
      row_vector.reshape(1, H), col_vector.reshape(1, H))
    return pl.pallas_call(
        part_results,
        out_shape=[jax.ShapeDtypeStruct((R, 32), f32), jax.ShapeDtypeStruct((C, 4), f32)],
        in_specs=[vmem],
        out_specs=[vmem, vmem],
    )(result)


def solution(mesh):
    in_specs = (
        P("row", "col", None),
        P("col", "row", None),
        P("row"),
        P("col"),
        P("row", "col"),
        P(),
        P(),
        P(),
    )
    out_specs = (P("row", "col"), P("col", "row"))
    return jax.shard_map(body, mesh=mesh, in_specs=in_specs, out_specs=out_specs, check_vma=False)
```
